32 devices in a mesh: mp: 4 (over x, core), fsdp: 8 (over z, y).
Axes of the slice: x: 2, y: 2, z: 4, core: 2. Of those that a mesh axis runs over, the one named last changes fastest.
Arguments:
- hidden_in: bfloat16 [4, 6144, 5120], P('mp', 'fsdp'), may hold values from -6 to 6
- gain_in: bfloat16 [4, 5120], P('mp'), may hold values from 0.099609375 to 1.8984375
- w_key: bfloat16 [4, 5120, 512], P('mp', 'fsdp'), may hold values from -0.078125 to 0.078125
- key_gain: bfloat16 [4, 128], P('mp'), may hold values from 0.099609375 to 1.8984375
- partner: int32 [4], replicated, may hold values from 0 to 3, as said below
Outputs:
- grad_key: float32 [4, 5120, 512], P('mp', 'fsdp')
- grad_key_gain: float32 [4, 128], P('mp')
- distill_loss: float32 [4], P('mp')
The draws below stay inside these ranges and needn't reach their ends.
Inputs may be any that keep to these rules, and one draw needn't show every extreme that they name: partner[m] differs from m.
All inputs are finite; a program needn't handle non-finite values.
Results may differ from the reference program's by a relative error of at most 0.0016.
Values may be sent and summed in bfloat16 or wider, within the bound.
No kernel may reach another device: no remote copies, remote signals or barrier semaphores. Data moves between devices by JAX's collectives and lax.ppermute only.
A program may use at most 128 MiB of HBM per device.

```python
import jax
import jax.numpy as jnp
from jax import lax

D = 5120
HD = 128
KW = 512
MODELS = 4
TOKENS = 6144


def draw_partner(key, part):
    key = jax.random.fold_in(key, 5)
    offsets = jax.random.randint(key, (MODELS,), 1, MODELS)
    return ((jnp.arange(MODELS) + offsets) % MODELS).astype(jnp.int32)


def spiked(drawn, own_key, source, target, blocks, factor):
    owner, partner = [(jnp.arange(drawn.shape[position]) // (drawn.shape[position] // blocks)).reshape([-1 if axis == position else 1 for axis in range(drawn.ndim)]) for position in (source, target)]
    chosen = jax.random.permutation(own_key, blocks)[partner]
    strong = (owner == chosen) | (owner == (partner + blocks // 2) % blocks)
    return jnp.where(strong, factor * drawn, drawn)


def shard_levels(stream_key, dims, cuts, smallest, high):
    loudness, own = 1.0, jax.random.fold_in(stream_key, 6)
    for axis_at, parts in cuts:
        draws = jnp.exp(jax.random.uniform(jax.random.fold_in(own, axis_at), (parts,), jnp.float32, smallest / len(cuts), high / len(cuts)))
        loudness = loudness * jnp.repeat(draws, dims[axis_at] // parts).reshape([-1 if axis == axis_at else 1 for axis in range(len(dims))])
    return loudness


def gaussian(own_key, extent, scale, reach, split=(), held_as=jnp.bfloat16):
    level = shard_levels(own_key, extent, split, -0.22, 0.18) if split else 1.0
    result = jax.random.normal(own_key, extent, jnp.float32) * scale * level
    return jnp.minimum(jnp.maximum(result, -reach), reach).astype(held_as)


def gaussian_with(own_key, shape, deviation, bound, cuts, heavy, dtype=jnp.bfloat16):
    array = deviation * jax.random.normal(own_key, shape, jnp.float32)
    if cuts:
        array = array * shard_levels(own_key, shape, cuts, -0.22, 0.18)
    return jnp.clip(spiked(array, jax.random.fold_in(own_key, 3), *heavy), -bound, bound).astype(dtype)


def setup_inputs(seed: int = 0) -> dict:
    arg_keys = jax.random.split(jax.random.key(seed), 6)
    return {
        "hidden_in": gaussian_with(arg_keys[0], (MODELS, TOKENS, D), 1.0, 6.0, ((0, 4), (1, 8)), (1, 2, 8, 2.0)),
        "gain_in": jnp.clip(1.0 + 0.18 * jax.random.normal(arg_keys[1], (MODELS, D), jnp.float32), 0.099609375, 1.8984375).astype(jnp.bfloat16),
        "w_key": gaussian(arg_keys[2], (MODELS, D, KW), D ** -0.5, 0.078125, ((0, 4), (1, 8))),
        "key_gain": jnp.clip(1.0 + 0.18 * jax.random.normal(arg_keys[3], (MODELS, HD), jnp.float32), 0.099609375, 1.8984375).astype(jnp.bfloat16),
        "partner": draw_partner(jax.random.fold_in(arg_keys[5], 71), 0),
    }


def norm_input(hidden, gain):
    values = hidden.astype(jnp.float32)
    scale = lax.rsqrt(lax.optimization_barrier(jnp.mean(values * values, axis=-1, keepdims=True)) + 1e-06)
    return (values * scale * gain.astype(jnp.float32)).astype(jnp.bfloat16)

def norm_keys(keys, gain):
    heads = keys.reshape(keys.shape[0], -1, gain.shape[0])
    inverse = lax.rsqrt(lax.optimization_barrier(jnp.mean(heads * heads, axis=-1, keepdims=True)) + 1e-06)
    return (heads, inverse, heads * inverse * gain.astype(jnp.float32))

def distill_terms(keys_student, keys_teacher, gain_student, gain_teacher):
    heads, inverse, out_student = norm_keys(keys_student, gain_student)
    unused_heads, unused_inverse, out_teacher = norm_keys(keys_teacher, gain_teacher)
    differ = out_student - out_teacher
    loss_sum = jnp.sum(differ * differ)
    upstream = differ / keys_student.shape[1]
    weighted = upstream * gain_student.astype(jnp.float32)
    inner = lax.optimization_barrier(jnp.sum(weighted * heads, axis=-1, keepdims=True))
    grad_heads = weighted * inverse - heads * inverse * inverse * inverse * inner / heads.shape[-1]
    grad_gain = lax.optimization_barrier(jnp.sum(upstream * heads * inverse, axis=(0, 1)))
    return (loss_sum, grad_heads.reshape(keys_student.shape).astype(jnp.bfloat16), grad_gain)

def reference(hidden_in, gain_in, w_key, key_gain, partner):
    grads = []
    gains = []
    losses = []
    for model in range(MODELS):
        teacher = partner[model]
        normed_student = norm_input(hidden_in[model], gain_in[model])
        normed_teacher = norm_input(hidden_in[model], gain_in[teacher])
        keys_student = jnp.dot(normed_student, w_key[model], preferred_element_type=jnp.float32)
        keys_teacher = jnp.dot(normed_teacher, w_key[teacher], preferred_element_type=jnp.float32)
        loss_sum, grad_keys, grad_gain = distill_terms(keys_student, keys_teacher, key_gain[model], key_gain[teacher])
        grads.append(jnp.dot(normed_student.T, grad_keys, preferred_element_type=jnp.float32))
        gains.append(grad_gain)
        losses.append(loss_sum / (TOKENS * KW))
    return (jnp.stack(grads), jnp.stack(gains), jnp.stack(losses))
```

```python
import functools

import jax
import jax.numpy as jnp
from jax import lax
from jax.experimental import pallas as pl
from jax.experimental.pallas import tpu as pltpu
from jax.sharding import PartitionSpec as P

EPS = 1e-06
NORM_TOKENS = 128
KEY_TOKENS = 256
VMEM_LIMIT = 24 * 1024 * 1024
ANY = pl.BlockSpec(memory_space=pl.ANY)
SMEM = pl.BlockSpec(memory_space=pltpu.SMEM)


def norm_kernel(order, rows, place_ref, hidden_ref, gain_ref, out_ref):
    values = hidden_ref[...].astype(jnp.float32)
    scale = lax.rsqrt(jnp.sum(values * values, axis=-1, keepdims=True) / values.shape[1] + EPS)
    line, member = lax.div(place_ref[0], 2), lax.rem(place_ref[0], 2)
    for at, (step, pair) in enumerate(order):
        owner = lax.rem(line + step, len(order) // 2) * 2 + lax.rem(member + pair, 2)
        source = pl.ds(pl.multiple_of(owner * rows, 128), rows)
        scaled = hidden_ref[:, source].astype(jnp.float32) * scale * gain_ref[:, source]
        out_ref[:, at * rows : (at + 1) * rows] = scaled.astype(jnp.bfloat16)


def normed_input(place, hidden, gain, order, rows):
    tokens, width = hidden.shape
    block = pl.BlockSpec((NORM_TOKENS, width), lambda i: (i, 0))
    return pl.pallas_call(
        functools.partial(norm_kernel, order, rows),
        grid=(tokens // NORM_TOKENS,),
        in_specs=[SMEM, block, pl.BlockSpec((1, width), lambda i: (0, 0))],
        out_specs=block,
        out_shape=jax.ShapeDtypeStruct(hidden.shape, jnp.bfloat16),
        compiler_params=pltpu.CompilerParams(vmem_limit_bytes=VMEM_LIMIT),
        cost_estimate=pl.CostEstimate(
            flops=6 * tokens * width, bytes_accessed=4 * tokens * width, transcendentals=tokens
        ),
        name="norm_input",
    )(place, hidden, gain)


def copy_blocks(sources, target, sems):
    copies, at = [], 0
    for i, source in enumerate(sources):
        rows = source.shape[0]
        copies.append(pltpu.make_async_copy(source, target.at[pl.ds(at, rows)], sems.at[i]))
        at += rows
    for copy in copies:
        copy.start()
    return copies


def load_weights(choice_ref, choices, target, sems):
    def load(sources):
        for copy in copy_blocks(sources, target, sems):
            copy.wait()

    if len(choices) == 1:
        load(choices[0])
    else:
        for i, sources in enumerate(choices):
            pl.when(choice_ref[0] == i)(functools.partial(load, sources))


def early_kernel(count, ways, adds, choice_ref, normed_ref, *refs):
    choices = [refs[i * count : (i + 1) * count] for i in range(ways)]
    before, (keys_ref, weights, sems) = refs[ways * count : -3], refs[-3:]

    @pl.when(pl.program_id(0) == 0)
    def _():
        load_weights(choice_ref, choices, weights, sems)

    keys = jnp.dot(normed_ref[...], weights[...], preferred_element_type=jnp.float32)
    keys_ref[...] = keys + before[0][...] if adds else keys


def early_keys(choice, normed, choices, first, before=None):
    ways, count, (rows, wide), tokens = len(choices), len(choices[0]), choices[0][0].shape, normed.shape[0]
    depth = count * rows
    keys = pl.BlockSpec((KEY_TOKENS, wide), lambda i: (i, 0))
    before = [] if before is None else [before]
    return pl.pallas_call(
        functools.partial(early_kernel, count, ways, bool(before)),
        grid=(tokens // KEY_TOKENS,),
        in_specs=[SMEM, pl.BlockSpec((KEY_TOKENS, depth), lambda i: (i, first // count))]
        + [ANY] * (ways * count)
        + [keys] * len(before),
        out_specs=keys,
        out_shape=jax.ShapeDtypeStruct((tokens, wide), jnp.float32),
        scratch_shapes=[pltpu.VMEM((depth, wide), jnp.bfloat16), pltpu.SemaphoreType.DMA((count,))],
        compiler_params=pltpu.CompilerParams(vmem_limit_bytes=VMEM_LIMIT),
        cost_estimate=pl.CostEstimate(
            flops=2 * tokens * depth * wide,
            bytes_accessed=2 * tokens * depth + 2 * depth * wide + 4 * tokens * wide,
            transcendentals=0,
        ),
        name="early_keys",
    )(choice, normed, *[block for one in choices for block in one], *before)


def late_kernel(counts, choice_ref, student_ref, teacher_ref, part_s_ref, part_t_ref, gain_s_ref, gain_t_ref, *refs):
    same, refs = refs[: counts[0]], refs[counts[0] :]
    choices, refs = [refs[i * counts[1] : (i + 1) * counts[1]] for i in range(3)], refs[3 * counts[1] :]
    grad_ref, stats_ref, w_s, w_t, sems_s, sems_t = refs
    step = pl.program_id(0)
    head, features = gain_s_ref.shape[1], part_s_ref.shape[1]

    @pl.when(step == 0)
    def _():
        load_weights(choice_ref, [same], w_s, sems_s)
        load_weights(choice_ref, choices, w_t, sems_t)

    keys_s = part_s_ref[...] + jnp.dot(student_ref[...], w_s[...], preferred_element_type=jnp.float32)
    keys_t = part_t_ref[...] + jnp.dot(teacher_ref[...], w_t[...], preferred_element_type=jnp.float32)
    gain_s, gain_t = gain_s_ref[...], gain_t_ref[...]
    gain_sum, loss_sum = 0.0, 0.0
    for at in range(0, features, head):
        heads, taught = keys_s[:, at : at + head], keys_t[:, at : at + head]
        inverse = lax.rsqrt(jnp.mean(heads * heads, axis=-1, keepdims=True) + EPS)
        inverse_t = lax.rsqrt(jnp.mean(taught * taught, axis=-1, keepdims=True) + EPS)
        differ = heads * inverse * gain_s - taught * inverse_t * gain_t
        upstream = differ * (1.0 / features)
        weighted = upstream * gain_s
        inner = jnp.sum(weighted * heads, axis=-1, keepdims=True)
        grad = weighted * inverse - heads * (inverse * inverse * inverse * inner / head)
        grad_ref[:, at : at + head] = grad.astype(jnp.bfloat16)
        gain_sum = gain_sum + jnp.sum(upstream * heads * inverse, axis=0, keepdims=True)
        loss_sum = loss_sum + jnp.sum(differ * differ, axis=0, keepdims=True)
    stats = jnp.concatenate([gain_sum, loss_sum, jnp.zeros((6, head), jnp.float32)], axis=0)

    @pl.when(step == 0)
    def _():
        stats_ref[...] = stats

    @pl.when(step != 0)
    def _():
        stats_ref[...] += stats


def late_keys(choice, student, teacher, part_s, part_t, gain_s, gain_t, same, choices, depth):
    counts, (tokens, wide), head = (len(same), len(choices[0])), part_s.shape, gain_s.shape[1]
    last = student.shape[1] // depth - 1
    token_block = pl.BlockSpec((KEY_TOKENS, depth), lambda i: (i, last))
    keys = pl.BlockSpec((KEY_TOKENS, wide), lambda i: (i, 0))
    gain = pl.BlockSpec((1, head), lambda i: (0, 0))
    return pl.pallas_call(
        functools.partial(late_kernel, counts),
        grid=(tokens // KEY_TOKENS,),
        in_specs=[SMEM, token_block, token_block, keys, keys, gain, gain] + [ANY] * (counts[0] + 3 * counts[1]),
        out_specs=[keys, pl.BlockSpec((8, head), lambda i: (0, 0))],
        out_shape=[jax.ShapeDtypeStruct((tokens, wide), jnp.bfloat16), jax.ShapeDtypeStruct((8, head), jnp.float32)],
        scratch_shapes=[pltpu.VMEM((depth, wide), jnp.bfloat16)] * 2
        + [pltpu.SemaphoreType.DMA((count,)) for count in counts],
        compiler_params=pltpu.CompilerParams(vmem_limit_bytes=VMEM_LIMIT),
        cost_estimate=pl.CostEstimate(
            flops=4 * tokens * depth * wide + 30 * tokens * wide,
            bytes_accessed=4 * tokens * depth + 4 * depth * wide + 10 * tokens * wide,
            transcendentals=2 * tokens * wide // head,
        ),
        name="late_keys",
    )(choice, student, teacher, part_s, part_t, gain_s, gain_t, *same, *[block for one in choices for block in one])


def grad_kernel(grad_ref, student_ref, out_ref):
    out_ref[0] = lax.dot_general(
        grad_ref[...], student_ref[...], (((0,), (0,)), ((), ())), preferred_element_type=jnp.float32
    ).astype(out_ref.dtype)


def grad_blocks(grad_keys, student, rows, first, stride, count, dtype):
    tokens, wide = grad_keys.shape
    return pl.pallas_call(
        grad_kernel,
        grid=(count,),
        in_specs=[
            pl.BlockSpec((tokens, wide), lambda i: (0, 0)),
            pl.BlockSpec((tokens, rows), lambda i: (0, first + stride * i)),
        ],
        out_specs=pl.BlockSpec((1, wide, rows), lambda i: (i, 0, 0)),
        out_shape=jax.ShapeDtypeStruct((count, wide, rows), dtype),
        compiler_params=pltpu.CompilerParams(vmem_limit_bytes=VMEM_LIMIT),
        cost_estimate=pl.CostEstimate(
            flops=2 * tokens * wide * rows * count,
            bytes_accessed=2 * tokens * (wide + rows * count) + 4 * count * wide * rows,
            transcendentals=0,
        ),
        name="grad_blocks",
    )(grad_keys, student)


def swap(value, axis, bit):
    return lax.ppermute(value, axis, [(i, i ^ bit) for i in range(lax.axis_size(axis))])


def fetch(value, step):
    size = lax.axis_size("fsdp")
    return lax.ppermute(value, "fsdp", [(i, (i - 2 * step) % size) for i in range(size)])


def after(value, *others):
    return lax.optimization_barrier((value,) + others)[0]


def phase(*values):
    return lax.optimization_barrier(values)


def local(hidden_in, gain_in, w_key, key_gain, partner):
    own_index = lax.axis_index("mp")
    teacher = partner[own_index]
    place = lax.axis_index("fsdp")
    lines = lax.axis_size("fsdp") // 2
    tok_rows, width = hidden_in.shape[1:]
    rows, features = w_key.shape[1:]
    head = key_gain.shape[1]

    far = lines // 2
    near = [step for step in range(1, lines) if step != far]
    order = [(0, 0), (0, 1)] + [(step, pair) for pair in range(2) for step in near] + [(far, 0), (far, 1)]
    place = place.astype(jnp.int32).reshape(1)
    own = w_key[0]

    gains_own = jnp.concatenate([gain_in, key_gain], axis=1)
    gains_beside = swap(gains_own, "mp", 2)
    gains_same = jnp.concatenate([gains_own, gains_beside], axis=0)
    gains_cross = swap(gains_same, "mp", 1)
    is_beside = teacher == own_index ^ 2
    gains_teacher = jnp.where(
        is_beside, gains_same[1:], jnp.where(teacher == own_index ^ 1, gains_cross[:1], gains_cross[1:])
    ).astype(jnp.float32)
    choice = jnp.where(is_beside, 0, jnp.where(teacher == own_index ^ 1, 1, 2)).astype(jnp.int32).reshape(1)
    same, other = {(0, 0): own}, {}
    for step in near:
        same[step, 0] = fetch(own, step)
    same[0, 1] = swap(own, "fsdp", 1)
    other[0, 0] = swap(after(own, gains_beside), "mp", 2)
    student = normed_input(place, hidden_in[0], gain_in.astype(jnp.float32), order, rows)
    other[0, 1] = swap(after(same[0, 1], student), "mp", 2)

    lead, *moved = phase(own, *[same[step, 0] for step in near], student)
    for step, block in zip(near, moved):
        same[step, 0] = block
        other[step, 0] = swap(block, "mp", 2)
        same[step, 1] = swap(block, "fsdp", 1)
    same[far, 0] = fetch(lead, far)
    hidden = after(hidden_in[0], lead)
    crossed = {}

    def cross(tables, keys):
        for table, name in tables:
            for key in keys:
                crossed[name, key] = swap(table[key], "mp", 1)

    both = ((same, "same"), (other, "other"))
    cross(both, [(0, 0), (0, 1)])
    normed = normed_input(place, hidden, gains_teacher[:, :width], order, rows)

    arrived = phase(
        same[far, 0],
        normed,
        *[same[step, 1] for step in near],
        *[other[step, 0] for step in near],
        *crossed.values(),
        other[0, 1],
    )
    same[far, 0], normed = arrived[:2]
    for i, step in enumerate(near):
        same[step, 1], other[step, 0] = arrived[2 + i], arrived[2 + len(near) + i]
    other[far, 0] = swap(same[far, 0], "mp", 2)
    same[far, 1] = swap(same[far, 0], "fsdp", 1)
    for i, step in enumerate(near):
        other[step, 1] = swap(other[step, 0], "fsdp", 1) if i % 2 == 0 else swap(same[step, 1], "mp", 2)
    cross(((same, "same"),), [(step, pair) for step in near for pair in range(2)])
    cross(((other, "other"),), [(step, 0) for step in near])

    def teachers(keys):
        return [[other[key] for key in keys]] + [[crossed[name, key] for key in keys] for name in ("same", "other")]

    part_s = early_keys(choice, student, [[same[key] for key in order[:-2]]], 0)
    part_t = early_keys(choice, normed, teachers(order[: 2 + len(near)]), 0)

    half = rows // 2
    upper = swap(after(same[far, 1][:half], part_s), "mp", 2)
    lower = swap(after(other[far, 0][half:], part_s), "fsdp", 1)
    cross(((other, "other"),), [(step, 1) for step in near])
    cross(((same, "same"),), [(far, 0), (far, 1)])
    cross(((other, "other"),), [(far, 0)])
    rest = order[2 + len(near) : -2]
    part_t = early_keys(choice, normed, teachers(rest), 2 + len(near), part_t)
    own_far = [same[far, 0], same[far, 1]]
    choices = [[other[far, 0], upper, lower], [crossed["same", (far, 0)], crossed["same", (far, 1)]]]
    choices.append([crossed["other", (far, 0)], swap(upper, "mp", 1), swap(lower, "mp", 1)])
    choices[1] = [choices[1][0], choices[1][1][:half], choices[1][1][half:]]
    grad_keys, stats = late_keys(
        choice,
        student,
        normed,
        part_s,
        part_t,
        key_gain.astype(jnp.float32),
        gains_teacher[:, width:],
        own_far,
        choices,
        2 * rows,
    )

    wide = features // 2
    at = order.index((far, 1))
    give_far = grad_blocks(grad_keys, student, rows, at, 1, 1, jnp.bfloat16)
    keep_far = grad_blocks(after(grad_keys, give_far), student, rows, at - 1, 1, 1, jnp.float32)
    given = [swap(give_far[0, i * wide : (i + 1) * wide], "fsdp", 1) for i in range(2)]
    sums = jnp.concatenate([stats[0], jnp.full((head,), jnp.sum(stats[1]))])
    bit = 2
    while bit < lax.axis_size("fsdp"):
        sums = sums + swap(sums, "fsdp", bit)
        bit *= 2
    pieces = grad_blocks(after(grad_keys, keep_far), student, rows, 2 + len(near), 1, len(near), jnp.bfloat16)
    given += [swap(after(pieces[i], given[0]), "fsdp", 1) for i in range(len(near))]
    keep = grad_blocks(after(grad_keys, pieces), student, rows, 2, 1, len(near), jnp.float32)
    ends = grad_blocks(after(grad_keys, keep), student, rows, 0, 1, 2, jnp.float32)
    last = swap(after(ends[1].astype(jnp.bfloat16), given[2]), "fsdp", 1)
    kept = [keep_far[0, i * wide : (i + 1) * wide] for i in range(2)] + [keep[i] for i in range(len(near))]
    arrived, before = [], []
    for step, mine, block in zip([far, far] + near, kept, given):
        summed = (mine + after(block, *before[-1:]).astype(jnp.float32)).astype(jnp.bfloat16)
        arrived.append(fetch(summed, -step))
        before.append(block)
    sums = sums + swap(after(sums, given[-1]), "fsdp", 1)
    total = ends[0] + last.astype(jnp.float32) + jnp.concatenate(arrived[:2], axis=0).astype(jnp.float32)
    for block in arrived[2:]:
        total = total + block.astype(jnp.float32)

    tokens_all = tok_rows * lax.axis_size("fsdp")
    distill_loss = (sums[head] / (tokens_all * features)).reshape(1)
    return (total.T[None], sums[None, :head], distill_loss)


def norm_input(hidden, gain):
    values = hidden.astype(jnp.float32)
    scale = lax.rsqrt(jnp.mean(values * values, axis=-1, keepdims=True) + EPS)
    return (values * scale * gain.astype(jnp.float32)).astype(jnp.bfloat16)


def norm_keys(keys, gain):
    heads = keys.reshape(keys.shape[0], -1, gain.shape[0])
    inverse = lax.rsqrt(jnp.mean(heads * heads, axis=-1, keepdims=True) + EPS)
    return (heads, inverse, heads * inverse * gain.astype(jnp.float32))


def plain(hidden_in, gain_in, w_key, key_gain, partner):
    partner_index = partner[lax.axis_index("mp")]
    every = [lax.all_gather(array, "mp", axis=0, tiled=True) for array in (w_key, gain_in, key_gain)]
    teach_w, teach_gain, teach_key_gain = [
        lax.dynamic_index_in_dim(array, partner_index, 0, keepdims=False) for array in every
    ]
    normed_student = norm_input(hidden_in[0], gain_in[0])
    normed_teacher = norm_input(hidden_in[0], teach_gain)
    keys_student, keys_teacher = [
        jnp.dot(normed, lax.all_gather(weight, "fsdp", axis=0, tiled=True), preferred_element_type=jnp.float32)
        for normed, weight in ((normed_student, w_key[0]), (normed_teacher, teach_w))
    ]
    heads, inverse, out_student = norm_keys(keys_student, key_gain[0])
    differ = out_student - norm_keys(keys_teacher, teach_key_gain)[2]
    upstream = differ / w_key.shape[2]
    weighted = upstream * key_gain[0].astype(jnp.float32)
    inner = jnp.sum(weighted * heads, axis=-1, keepdims=True)
    grad_heads = weighted * inverse - heads * inverse * inverse * inverse * inner / heads.shape[-1]
    grad_keys = grad_heads.reshape(keys_student.shape).astype(jnp.bfloat16)
    grad_gain = jnp.sum(upstream * heads * inverse, axis=(0, 1))
    loss_total, gain_total = lax.psum((jnp.sum(differ * differ), grad_gain), "fsdp")
    tokens_all = hidden_in.shape[1] * lax.axis_size("fsdp")
    grad = lax.dot_general(
        normed_student, grad_keys, (((0,), (0,)), ((), ())), preferred_element_type=jnp.float32
    )
    grad_rows = lax.psum_scatter(grad, "fsdp", scatter_dimension=0, tiled=True)
    distill_loss = (loss_total / (tokens_all * w_key.shape[2])).reshape(1)
    return (grad_rows[None], gain_total[None], distill_loss)


def step(hidden_in, gain_in, w_key, key_gain, partner):
    body = plain if w_key.shape[1] % 128 else local
    return body(hidden_in, gain_in, w_key, key_gain, partner)


def solution(mesh):
    return jax.shard_map(
        step,
        mesh=mesh,
        in_specs=(P("mp", "fsdp", None), P("mp", None), P("mp", "fsdp", None), P("mp", None), P()),
        out_specs=(P("mp", "fsdp", None), P("mp", None), P("mp")),
        check_vma=False,
    )
```

```python
import functools

import jax
import jax.numpy as jnp
from jax import lax
from jax.experimental import pallas as pl
from jax.experimental.pallas import tpu as pltpu
from jax.sharding import PartitionSpec as P

EPS = 1e-06
NORM_TOKENS = 128
KEY_TOKENS = 256
VMEM_LIMIT = 24 * 1024 * 1024
SHORT = pl.CostEstimate(flops=1, bytes_accessed=1, transcendentals=0)
ANY = pl.BlockSpec(memory_space=pl.ANY)
SMEM = pl.BlockSpec(memory_space=pltpu.SMEM)


def norm_kernel(order, rows, place_ref, hidden_ref, gain_ref, out_ref):
    values = hidden_ref[...].astype(jnp.float32)
    scale = lax.rsqrt(jnp.sum(values * values, axis=-1, keepdims=True) / values.shape[1] + EPS)
    line, member = lax.div(place_ref[0], 2), lax.rem(place_ref[0], 2)
    for at, (step, pair) in enumerate(order):
        owner = lax.rem(line + step, len(order) // 2) * 2 + lax.rem(member + pair, 2)
        source = pl.ds(pl.multiple_of(owner * rows, 128), rows)
        scaled = hidden_ref[:, source].astype(jnp.float32) * scale * gain_ref[:, source]
        out_ref[:, at * rows : (at + 1) * rows] = scaled.astype(jnp.bfloat16)


def normed_input(place, hidden, gain, order, rows):
    tokens, width = hidden.shape
    block = pl.BlockSpec((NORM_TOKENS, width), lambda i: (i, 0))
    return pl.pallas_call(
        functools.partial(norm_kernel, order, rows),
        grid=(tokens // NORM_TOKENS,),
        in_specs=[SMEM, block, pl.BlockSpec((1, width), lambda i: (0, 0))],
        out_specs=block,
        out_shape=pltpu.HBM(hidden.shape, jnp.bfloat16),
        compiler_params=pltpu.CompilerParams(vmem_limit_bytes=VMEM_LIMIT),
        cost_estimate=SHORT,
        name="norm_input",
    )(place, in_hbm(hidden), gain)


def copy_blocks(sources, target, sems):
    copies, at = [], 0
    for i, source in enumerate(sources):
        rows = source.shape[0]
        copies.append(pltpu.make_async_copy(source, target.at[pl.ds(at, rows)], sems.at[i]))
        at += rows
    for copy in copies:
        copy.start()
    return copies


def load_weights(choice_ref, choices, target, sems):
    def load(sources):
        for copy in copy_blocks(sources, target, sems):
            copy.wait()

    if len(choices) == 1:
        load(choices[0])
    else:
        for i, sources in enumerate(choices):
            pl.when(choice_ref[0] == i)(functools.partial(load, sources))


def in_hbm(array):
    return pltpu.with_memory_space_constraint(array, pltpu.HBM)


def split(refs, counts):
    lists = []
    for count in counts:
        lists.append(refs[:count])
        refs = refs[count:]
    return lists, refs


def pack_kernel(counts, choice_ref, *refs):
    choices, (out_ref, sems) = split(refs, counts)
    load_weights(choice_ref, choices, out_ref, sems)


def pack(choice, *choices):
    rows, wide = sum(block.shape[0] for block in choices[0]), choices[0][0].shape[1]
    counts = [len(blocks) for blocks in choices]
    return pl.pallas_call(
        functools.partial(pack_kernel, counts),
        in_specs=[SMEM] + [ANY] * sum(counts),
        out_specs=pl.BlockSpec(memory_space=pltpu.VMEM),
        out_shape=jax.ShapeDtypeStruct((rows, wide), choices[0][0].dtype),
        scratch_shapes=[pltpu.SemaphoreType.DMA((max(counts),))],
        compiler_params=pltpu.CompilerParams(vmem_limit_bytes=VMEM_LIMIT),
        cost_estimate=SHORT,
        name="pack_blocks",
    )(choice, *[block for blocks in choices for block in blocks])


def early_kernel(counts, adds, choice_ref, normed_ref, *refs):
    choices, refs = split(refs, counts)
    before, (keys_ref, weights, sems) = refs[:-3], refs[-3:]

    @pl.when(pl.program_id(0) == 0)
    def _():
        load_weights(choice_ref, choices, weights, sems)

    keys = jnp.dot(normed_ref[...], weights[...], preferred_element_type=jnp.float32)
    keys_ref[...] = keys + before[0][...] if adds else keys


def early_keys(choice, normed, choices, first, before=None):
    depth, wide, tokens = sum(block.shape[0] for block in choices[0]), choices[0][0].shape[1], normed.shape[0]
    counts = [len(blocks) for blocks in choices]
    keys = pl.BlockSpec((KEY_TOKENS, wide), lambda i: (i, 0))
    before = [] if before is None else [before]
    return pl.pallas_call(
        functools.partial(early_kernel, counts, bool(before)),
        grid=(tokens // KEY_TOKENS,),
        in_specs=[SMEM, pl.BlockSpec((KEY_TOKENS, depth), lambda i: (i, first // depth))]
        + [ANY] * sum(counts)
        + [keys] * len(before),
        out_specs=keys,
        out_shape=jax.ShapeDtypeStruct((tokens, wide), jnp.float32),
        scratch_shapes=[pltpu.VMEM((depth, wide), jnp.bfloat16), pltpu.SemaphoreType.DMA((max(counts),))],
        compiler_params=pltpu.CompilerParams(vmem_limit_bytes=VMEM_LIMIT),
        cost_estimate=SHORT,
        name="early_keys",
    )(choice, in_hbm(normed), *[block for blocks in choices for block in blocks], *before)


def late_kernel(
    counts, choice_ref, student_ref, teacher_ref, part_s_ref, part_t_ref, gain_s_ref, gain_t_ref, *refs
):
    (same, *choices), (grad_ref, stats_ref, w_s, w_t, sems_s, sems_t) = split(refs, counts)
    step, head, features = pl.program_id(0), gain_s_ref.shape[1], part_s_ref.shape[1]

    @pl.when(step == 0)
    def _():
        own = copy_blocks(same, w_s, sems_s)
        load_weights(choice_ref, choices, w_t, sems_t)
        for copy in own:
            copy.wait()

    keys_s = part_s_ref[...] + jnp.dot(student_ref[...], w_s[...], preferred_element_type=jnp.float32)
    keys_t = part_t_ref[...] + jnp.dot(teacher_ref[...], w_t[...], preferred_element_type=jnp.float32)
    gain_s, gain_t = gain_s_ref[...], gain_t_ref[...]
    gain_sum, loss_sum = 0.0, 0.0
    for at in range(0, keys_s.shape[1], head):
        heads, taught = keys_s[:, at : at + head], keys_t[:, at : at + head]
        inverse = lax.rsqrt(jnp.mean(heads * heads, axis=-1, keepdims=True) + EPS)
        inverse_t = lax.rsqrt(jnp.mean(taught * taught, axis=-1, keepdims=True) + EPS)
        differ = heads * inverse * gain_s - taught * inverse_t * gain_t
        upstream = differ * (1.0 / features)
        weighted = upstream * gain_s
        inner = jnp.sum(weighted * heads, axis=-1, keepdims=True)
        grad = weighted * inverse - heads * (inverse * inverse * inverse * inner / head)
        grad_ref[:, at : at + head] = grad.astype(jnp.bfloat16)
        gain_sum = gain_sum + jnp.sum(upstream * heads * inverse, axis=0, keepdims=True)
        loss_sum = loss_sum + jnp.sum(differ * differ, axis=0, keepdims=True)
    stats = jnp.concatenate([gain_sum, loss_sum, jnp.zeros((6, head), jnp.float32)], axis=0)

    @pl.when(step == 0)
    def _():
        stats_ref[...] = stats

    @pl.when(step != 0)
    def _():
        stats_ref[...] += stats


def late_keys(choice, student, teacher, part_s, part_t, gain_s, gain_t, same, choices):
    counts, (tokens, wide), head = [len(same)] + [len(blocks) for blocks in choices], part_s.shape, gain_s.shape[1]
    depth = sum(block.shape[0] for block in same)
    last = student.shape[1] // depth - 1
    token_block = pl.BlockSpec((KEY_TOKENS, depth), lambda i: (i, last))
    keys = pl.BlockSpec((KEY_TOKENS, wide), lambda i: (i, 0))
    gain = pl.BlockSpec((1, head), lambda i: (0, 0))
    return pl.pallas_call(
        functools.partial(late_kernel, counts),
        grid=(tokens // KEY_TOKENS,),
        in_specs=[SMEM, token_block, token_block, keys, keys, gain, gain] + [ANY] * sum(counts),
        out_specs=[keys, pl.BlockSpec((8, head), lambda i: (0, 0))],
        out_shape=[jax.ShapeDtypeStruct((tokens, wide), jnp.bfloat16), jax.ShapeDtypeStruct((8, head), jnp.float32)],
        scratch_shapes=[pltpu.VMEM((depth, wide), jnp.bfloat16)] * 2
        + [pltpu.SemaphoreType.DMA((count,)) for count in (counts[0], max(counts[1:]))],
        compiler_params=pltpu.CompilerParams(vmem_limit_bytes=VMEM_LIMIT),
        cost_estimate=SHORT,
        name="late_keys",
    )(
        choice,
        in_hbm(student),
        in_hbm(teacher),
        part_s,
        part_t,
        gain_s,
        gain_t,
        *same,
        *[block for blocks in choices for block in blocks],
    )


def grad_kernel(grad_ref, student_ref, out_ref):
    out_ref[0] = lax.dot_general(
        grad_ref[...], student_ref[...], (((0,), (0,)), ((), ())), preferred_element_type=jnp.float32
    ).astype(out_ref.dtype)


def grad_blocks(grad_keys, student, rows, blocks, dtype):
    (tokens, wide), count, first = grad_keys.shape, len(blocks), blocks[0]
    stride = blocks[1] - first if count > 1 else 1
    return pl.pallas_call(
        grad_kernel,
        grid=(count,),
        in_specs=[
            pl.BlockSpec((tokens, wide), lambda i: (0, 0)),
            pl.BlockSpec((tokens, rows), lambda i: (0, first + stride * i)),
        ],
        out_specs=pl.BlockSpec((1, wide, rows), lambda i: (i, 0, 0)),
        out_shape=jax.ShapeDtypeStruct((count, wide, rows), dtype),
        compiler_params=pltpu.CompilerParams(vmem_limit_bytes=VMEM_LIMIT),
        cost_estimate=SHORT,
        name="grad_blocks",
    )(grad_keys, in_hbm(student))


def swap(value, axis, bit):
    return lax.ppermute(value, axis, [(i, i ^ bit) for i in range(lax.axis_size(axis))])


def fetch(value, step):
    size = lax.axis_size("fsdp")
    return lax.ppermute(value, "fsdp", [(i, (i - 2 * step) % size) for i in range(size)])


def after(value, *others):
    return lax.optimization_barrier((value,) + others)[0]


def phase(*values):
    return lax.optimization_barrier(values)


def local(hidden_in, gain_in, w_key, key_gain, partner):
    own_index = lax.axis_index("mp")
    teacher = partner[own_index]
    place = lax.axis_index("fsdp")
    lines = lax.axis_size("fsdp") // 2
    tok_rows, width = hidden_in.shape[1:]
    rows, features = w_key.shape[1:]
    head = key_gain.shape[1]

    far = lines // 2
    near = [step for step in range(1, lines) if step != far]
    order = [(0, 0), (0, 1)] + [(step, 0) for step in near]
    order += [(step, 1) for step in near[:-1]] + [(far, 0), (near[-1], 1), (far, 1)]
    place = place.astype(jnp.int32).reshape(1)
    own = w_key[0]

    same, other = {(0, 0): own}, {}
    for step in near:
        same[step, 0] = fetch(own, step)
    same[0, 1] = swap(own, "fsdp", 1)
    other[0, 0] = swap(own, "mp", 2)
    other[0, 1] = swap(same[0, 1], "mp", 2)
    same[far, 0] = fetch(after(own, same[near[0], 0]), far)
    student = normed_input(place, hidden_in[0], gain_in.astype(jnp.float32), order, rows)
    gains_own = jnp.concatenate([gain_in, key_gain], axis=1)
    gains_beside = swap(gains_own, "mp", 2)
    student, gains_beside, other[0, 0], other[0, 1], *moved = phase(
        student, gains_beside, other[0, 0], other[0, 1], *[same[step, 0] for step in near]
    )
    gains_same = jnp.concatenate([gains_own, gains_beside], axis=0)
    gains_cross = swap(gains_same, "mp", 1)
    is_beside = teacher == own_index ^ 2
    gains_teacher = jnp.where(
        is_beside, gains_same[1:], jnp.where(teacher == own_index ^ 1, gains_cross[:1], gains_cross[1:])
    ).astype(jnp.float32)
    choice = jnp.where(is_beside, 0, 1).astype(jnp.int32).reshape(1)
    offer = jnp.where(partner[own_index ^ 1] == own_index, 0, 1).astype(jnp.int32).reshape(1)
    normed = normed_input(place, after(hidden_in[0], student), gains_teacher[:, :width], order, rows)

    for step, block in zip(near, moved):
        same[step, 0] = block
        other[step, 0] = swap(block, "mp", 2)
        same[step, 1] = swap(block, "fsdp", 1)

    arrived = phase(
        same[far, 0],
        normed,
        *[same[step, 1] for step in near],
        *[other[step, 0] for step in near],
    )
    same[far, 0], normed = arrived[:2]
    for i, step in enumerate(near):
        same[step, 1], other[step, 0] = arrived[2 + i], arrived[2 + len(near) + i]

    def cross(mine, beside, *wait):
        return swap(pack(after(offer, *wait), mine, beside), "mp", 1)

    first, second, end = order[: 2 + len(near)], order[2 + len(near) : -2], near[-1]
    half = rows // 2
    lead = after(same[0, 1], same[end, 1])
    other[far, 0] = swap(same[far, 0], "mp", 2)
    for step in near[:-1]:
        other[step, 1] = swap(other[step, 0], "fsdp", 1)
    upper = fetch(lead[:half], far)
    part_s = early_keys(choice, student, [[same[key] for key in first + second]], 0)
    crossed = cross([same[key] for key in first], [other[key] for key in first])
    arrived = phase(lead, other[far, 0], upper, part_s, crossed, *[other[step, 1] for step in near[:-1]])
    lead, other[far, 0], upper, part_s, crossed = arrived[:5]
    for step, block in zip(near[:-1], arrived[5:]):
        other[step, 1] = block

    lower = fetch(lead[half:], far)
    other[end, 1] = swap(after(same[end, 1], upper), "mp", 2)
    other[far, 1] = swap(other[far, 0], "fsdp", 1)
    part_t = early_keys(choice, normed, [[other[key] for key in first], [crossed]], 0)
    mine, beside = [same[end, 1], upper, lower], [other[end, 1], other[far, 1]]
    last = cross(mine, beside, part_t)
    crossed = cross([same[key] for key in second], [other[key] for key in second])
    part_t = early_keys(choice, normed, [[other[key] for key in second], [crossed]], len(first) * rows, part_t)
    grad_keys, stats = late_keys(
        choice,
        student,
        normed,
        part_s,
        part_t,
        key_gain.astype(jnp.float32),
        gains_teacher[:, width:],
        mine,
        [beside, [last]],
    )

    def grads(keys, dtype, *wait):
        return grad_blocks(after(grad_keys, *wait), student, rows, [order.index(key) for key in keys], dtype)

    wide = features // 2
    give_far = grads([(far, 1)], jnp.bfloat16)
    given = [swap(give_far[0, at : at + wide], "fsdp", 1) for at in (0, wide)]
    keep_far = grads([(far, 0)], jnp.float32, given[0])
    sums = jnp.concatenate([stats[0], jnp.full((head,), jnp.sum(stats[1]))])
    bit = 2
    while bit < lax.axis_size("fsdp"):
        sums = sums + swap(sums, "fsdp", bit)
        bit *= 2
    pieces = grads([(step, 1) for step in near], jnp.bfloat16, keep_far)
    keep = grads([(step, 0) for step in near], jnp.float32, pieces)
    ends = grads([(0, 0), (0, 1)], jnp.float32, keep)
    kept = [keep_far[0, at : at + wide] for at in (0, wide)] + [keep[i] for i in range(len(near))]
    arrived = []
    for at, step in enumerate([far, far] + near):
        if at >= 2:
            ready = given[0] if at == 2 else arrived[at - 3]
            given.append(swap(after(pieces[at - 2], ready), "fsdp", 1))
        mine, block = phase(kept[at], given[at])
        summed = (mine + block.astype(jnp.float32)).astype(jnp.bfloat16)
        arrived.append(fetch(after(summed, sums if at < 2 else arrived[at - 2]), -step))
    last = swap(after(ends[1].astype(jnp.bfloat16), given[2], arrived[1]), "fsdp", 1)
    sums = sums + swap(after(sums, given[-1]), "fsdp", 1)
    total = ends[0] + last.astype(jnp.float32) + jnp.concatenate(arrived[:2], axis=0).astype(jnp.float32)
    for block in arrived[2:]:
        total = total + block.astype(jnp.float32)

    tokens_all = tok_rows * lax.axis_size("fsdp")
    distill_loss = (sums[head] / (tokens_all * features)).reshape(1)
    return (total.T[None], sums[None, :head], distill_loss)


def norm_input(hidden, gain):
    values = hidden.astype(jnp.float32)
    scale = lax.rsqrt(jnp.mean(values * values, axis=-1, keepdims=True) + EPS)
    return (values * scale * gain.astype(jnp.float32)).astype(jnp.bfloat16)


def norm_keys(keys, gain):
    heads = keys.reshape(keys.shape[0], -1, gain.shape[0])
    inverse = lax.rsqrt(jnp.mean(heads * heads, axis=-1, keepdims=True) + EPS)
    return (heads, inverse, heads * inverse * gain.astype(jnp.float32))


def plain(hidden_in, gain_in, w_key, key_gain, partner):
    partner_index = partner[lax.axis_index("mp")]
    every = [lax.all_gather(array, "mp", axis=0, tiled=True) for array in (w_key, gain_in, key_gain)]
    teach_w, teach_gain, teach_key_gain = [
        lax.dynamic_index_in_dim(array, partner_index, 0, keepdims=False) for array in every
    ]
    normed_student = norm_input(hidden_in[0], gain_in[0])
    normed_teacher = norm_input(hidden_in[0], teach_gain)
    keys_student, keys_teacher = [
        jnp.dot(normed, lax.all_gather(weight, "fsdp", axis=0, tiled=True), preferred_element_type=jnp.float32)
        for normed, weight in ((normed_student, w_key[0]), (normed_teacher, teach_w))
    ]
    heads, inverse, out_student = norm_keys(keys_student, key_gain[0])
    differ = out_student - norm_keys(keys_teacher, teach_key_gain)[2]
    upstream = differ / w_key.shape[2]
    weighted = upstream * key_gain[0].astype(jnp.float32)
    inner = jnp.sum(weighted * heads, axis=-1, keepdims=True)
    grad_heads = weighted * inverse - heads * inverse * inverse * inverse * inner / heads.shape[-1]
    grad_keys = grad_heads.reshape(keys_student.shape).astype(jnp.bfloat16)
    grad_gain = jnp.sum(upstream * heads * inverse, axis=(0, 1))
    loss_total, gain_total = lax.psum((jnp.sum(differ * differ), grad_gain), "fsdp")
    tokens_all = hidden_in.shape[1] * lax.axis_size("fsdp")
    grad = lax.dot_general(
        normed_student, grad_keys, (((0,), (0,)), ((), ())), preferred_element_type=jnp.float32
    )
    grad_rows = lax.psum_scatter(grad, "fsdp", scatter_dimension=0, tiled=True)
    distill_loss = (loss_total / (tokens_all * w_key.shape[2])).reshape(1)
    return (grad_rows[None], gain_total[None], distill_loss)


def step(hidden_in, gain_in, w_key, key_gain, partner):
    body = plain if w_key.shape[1] % 128 else local
    return body(hidden_in, gain_in, w_key, key_gain, partner)


def solution(mesh):
    return jax.shard_map(
        step,
        mesh=mesh,
        in_specs=(P("mp", "fsdp", None), P("mp", None), P("mp", "fsdp", None), P("mp", None), P()),
        out_specs=(P("mp", "fsdp", None), P("mp", None), P("mp")),
        check_vma=False,
    )
```

```python
import functools

import jax
import jax.numpy as jnp
from jax import lax
from jax.experimental import pallas as pl
from jax.experimental.pallas import tpu as pltpu
from jax.sharding import PartitionSpec as P

EPS = 1e-06
NORM_TOKENS = 128
KEY_TOKENS = 256
VMEM_LIMIT = 24 * 1024 * 1024
SHORT = pl.CostEstimate(flops=1, bytes_accessed=1, transcendentals=0)
ANY = pl.BlockSpec(memory_space=pl.ANY)
SMEM = pl.BlockSpec(memory_space=pltpu.SMEM)


def norm_kernel(order, rows, place_ref, hidden_ref, gain_ref, out_ref):
    values = hidden_ref[...].astype(jnp.float32)
    scale = lax.rsqrt(jnp.sum(values * values, axis=-1, keepdims=True) / values.shape[1] + EPS)
    line, member = lax.div(place_ref[0], 2), lax.rem(place_ref[0], 2)
    for at, (step, pair) in enumerate(order):
        owner = lax.rem(line + step, len(order) // 2) * 2 + lax.rem(member + pair, 2)
        source = pl.ds(pl.multiple_of(owner * rows, 128), rows)
        scaled = hidden_ref[:, source].astype(jnp.float32) * scale * gain_ref[:, source]
        out_ref[:, at * rows : (at + 1) * rows] = scaled.astype(jnp.bfloat16)


def normed_input(place, hidden, gain, order, rows):
    tokens, width = hidden.shape
    block = pl.BlockSpec((NORM_TOKENS, width), lambda i: (i, 0))
    return pl.pallas_call(
        functools.partial(norm_kernel, order, rows),
        grid=(tokens // NORM_TOKENS,),
        in_specs=[SMEM, block, pl.BlockSpec((1, width), lambda i: (0, 0))],
        out_specs=block,
        out_shape=pltpu.HBM(hidden.shape, jnp.bfloat16),
        compiler_params=pltpu.CompilerParams(vmem_limit_bytes=VMEM_LIMIT),
        cost_estimate=SHORT,
        name="norm_input",
    )(place, in_hbm(hidden), gain)


def copy_blocks(sources, target, sems):
    copies, at = [], 0
    for i, source in enumerate(sources):
        rows = source.shape[0]
        copies.append(pltpu.make_async_copy(source, target.at[pl.ds(at, rows)], sems.at[i]))
        at += rows
    for copy in copies:
        copy.start()
    return copies


def load_weights(choice_ref, choices, target, sems):
    def load(sources):
        for copy in copy_blocks(sources, target, sems):
            copy.wait()

    if len(choices) == 1:
        load(choices[0])
    else:
        for i, sources in enumerate(choices):
            pl.when(choice_ref[0] == i)(functools.partial(load, sources))


def in_hbm(array):
    return pltpu.with_memory_space_constraint(array, pltpu.HBM)


def split(refs, counts):
    lists = []
    for count in counts:
        lists.append(refs[:count])
        refs = refs[count:]
    return lists, refs


def pack_kernel(counts, choice_ref, *refs):
    choices, (out_ref, sems) = split(refs, counts)
    load_weights(choice_ref, choices, out_ref, sems)


def pack(choice, *choices):
    rows, wide = sum(block.shape[0] for block in choices[0]), choices[0][0].shape[1]
    counts = [len(blocks) for blocks in choices]
    return pl.pallas_call(
        functools.partial(pack_kernel, counts),
        in_specs=[SMEM] + [ANY] * sum(counts),
        out_specs=pl.BlockSpec(memory_space=pltpu.VMEM),
        out_shape=jax.ShapeDtypeStruct((rows, wide), choices[0][0].dtype),
        scratch_shapes=[pltpu.SemaphoreType.DMA((max(counts),))],
        compiler_params=pltpu.CompilerParams(vmem_limit_bytes=VMEM_LIMIT),
        cost_estimate=SHORT,
        name="pack_blocks",
    )(choice, *[block for blocks in choices for block in blocks])


def early_kernel(counts, adds, choice_ref, normed_ref, *refs):
    choices, refs = split(refs, counts)
    before, (keys_ref, weights, sems) = refs[:-3], refs[-3:]

    @pl.when(pl.program_id(0) == 0)
    def _():
        load_weights(choice_ref, choices, weights, sems)

    keys = jnp.dot(normed_ref[...], weights[...], preferred_element_type=jnp.float32)
    keys_ref[...] = keys + before[0][...] if adds else keys


def early_keys(choice, normed, choices, first, before=None):
    depth, wide, tokens = sum(block.shape[0] for block in choices[0]), choices[0][0].shape[1], normed.shape[0]
    counts = [len(blocks) for blocks in choices]
    keys = pl.BlockSpec((KEY_TOKENS, wide), lambda i: (i, 0))
    before = [] if before is None else [before]
    return pl.pallas_call(
        functools.partial(early_kernel, counts, bool(before)),
        grid=(tokens // KEY_TOKENS,),
        in_specs=[SMEM, pl.BlockSpec((KEY_TOKENS, depth), lambda i: (i, first // depth))]
        + [ANY] * sum(counts)
        + [keys] * len(before),
        out_specs=keys,
        out_shape=jax.ShapeDtypeStruct((tokens, wide), jnp.float32),
        scratch_shapes=[pltpu.VMEM((depth, wide), jnp.bfloat16), pltpu.SemaphoreType.DMA((max(counts),))],
        compiler_params=pltpu.CompilerParams(vmem_limit_bytes=VMEM_LIMIT),
        cost_estimate=SHORT,
        name="early_keys",
    )(choice, in_hbm(normed), *[block for blocks in choices for block in blocks], *before)


def late_kernel(counts, choice_ref, student_ref, teacher_ref, part_s_ref, part_t_ref, gain_s_ref, gain_t_ref, *refs):
    (same, *choices), refs = split(refs, counts)
    keep_of_ref, give_of_ref, grad_ref, stats_ref, keep_ref, give_ref, w_s, w_t, sems_s, sems_t = refs
    step = pl.program_id(0)
    head, features = gain_s_ref.shape[1], part_s_ref.shape[1]

    @pl.when(step == 0)
    def _():
        own = copy_blocks(same, w_s, sems_s)
        load_weights(choice_ref, choices, w_t, sems_t)
        for copy in own:
            copy.wait()

    keys_s = part_s_ref[...] + jnp.dot(student_ref[...], w_s[...], preferred_element_type=jnp.float32)
    keys_t = part_t_ref[...] + jnp.dot(teacher_ref[...], w_t[...], preferred_element_type=jnp.float32)
    gain_s, gain_t = gain_s_ref[...], gain_t_ref[...]
    gain_sum, loss_sum = 0.0, 0.0
    tokens = pl.ds(pl.multiple_of(step * keys_s.shape[0], 256), keys_s.shape[0])
    for at in range(0, features, head):
        heads, taught = keys_s[:, at : at + head], keys_t[:, at : at + head]
        inverse = lax.rsqrt(jnp.mean(heads * heads, axis=-1, keepdims=True) + EPS)
        inverse_t = lax.rsqrt(jnp.mean(taught * taught, axis=-1, keepdims=True) + EPS)
        differ = heads * inverse * gain_s - taught * inverse_t * gain_t
        upstream = differ * (1.0 / features)
        weighted = upstream * gain_s
        inner = jnp.sum(weighted * heads, axis=-1, keepdims=True)
        grad = weighted * inverse - heads * (inverse * inverse * inverse * inner / head)
        grad_ref[tokens, at : at + head] = grad.astype(jnp.bfloat16)
        gain_sum = gain_sum + jnp.sum(upstream * heads * inverse, axis=0, keepdims=True)
        loss_sum = loss_sum + jnp.sum(differ * differ, axis=0, keepdims=True)
    stats = jnp.concatenate([gain_sum, loss_sum, jnp.zeros((6, head), jnp.float32)], axis=0)

    @pl.when(step == 0)
    def _():
        stats_ref[...] = stats

    @pl.when(step != 0)
    def _():
        stats_ref[...] += stats

    @pl.when(step == pl.num_programs(0) - 1)
    def _():
        for block_ref, out_ref in ((give_of_ref, give_ref), (keep_of_ref, keep_ref)):
            out_ref[...] = lax.dot_general(
                grad_ref[...], block_ref[...], (((0,), (0,)), ((), ())), preferred_element_type=jnp.float32
            ).astype(out_ref.dtype)


def late_keys(choice, student, teacher, part_s, part_t, gain_s, gain_t, same, choices, rows, far):
    counts, (tokens, wide), head = [len(same)] + [len(blocks) for blocks in choices], part_s.shape, gain_s.shape[1]
    depth = sum(block.shape[0] for block in same)
    last = student.shape[1] // depth - 1
    token_block = pl.BlockSpec((KEY_TOKENS, depth), lambda i: (i, last))
    keys = pl.BlockSpec((KEY_TOKENS, wide), lambda i: (i, 0))
    gain = pl.BlockSpec((1, head), lambda i: (0, 0))
    far_blocks = [pl.BlockSpec((tokens, rows), lambda i, at=at: (0, at)) for at in far]
    outs = [
        jax.ShapeDtypeStruct((tokens, wide), jnp.bfloat16),
        jax.ShapeDtypeStruct((8, head), jnp.float32),
        jax.ShapeDtypeStruct((wide, rows), jnp.float32),
        jax.ShapeDtypeStruct((wide, rows), jnp.bfloat16),
    ]
    student, teacher = in_hbm(student), in_hbm(teacher)
    return pl.pallas_call(
        functools.partial(late_kernel, counts),
        grid=(tokens // KEY_TOKENS,),
        in_specs=[SMEM, token_block, token_block, keys, keys, gain, gain] + [ANY] * sum(counts) + far_blocks,
        out_specs=[pl.BlockSpec(out.shape, lambda i: (0, 0)) for out in outs],
        out_shape=outs,
        scratch_shapes=[pltpu.VMEM((depth, wide), jnp.bfloat16)] * 2
        + [pltpu.SemaphoreType.DMA((count,)) for count in (counts[0], max(counts[1:]))],
        compiler_params=pltpu.CompilerParams(vmem_limit_bytes=VMEM_LIMIT),
        cost_estimate=SHORT,
        name="late_keys",
    )(
        choice,
        student,
        teacher,
        part_s,
        part_t,
        gain_s,
        gain_t,
        *same,
        *[block for blocks in choices for block in blocks],
        student,
        student,
    )


def grad_kernel(grad_ref, student_ref, out_ref):
    out_ref[0] = lax.dot_general(
        grad_ref[...], student_ref[...], (((0,), (0,)), ((), ())), preferred_element_type=jnp.float32
    ).astype(out_ref.dtype)


def grad_blocks(grad_keys, student, rows, blocks, dtype):
    (tokens, wide), count, first = grad_keys.shape, len(blocks), blocks[0]
    stride = blocks[1] - first if count > 1 else 1
    return pl.pallas_call(
        grad_kernel,
        grid=(count,),
        in_specs=[
            pl.BlockSpec((tokens, wide), lambda i: (0, 0)),
            pl.BlockSpec((tokens, rows), lambda i: (0, first + stride * i)),
        ],
        out_specs=pl.BlockSpec((1, wide, rows), lambda i: (i, 0, 0)),
        out_shape=jax.ShapeDtypeStruct((count, wide, rows), dtype),
        compiler_params=pltpu.CompilerParams(vmem_limit_bytes=VMEM_LIMIT),
        cost_estimate=SHORT,
        name="grad_blocks",
    )(grad_keys, in_hbm(student))


def swap(value, axis, bit):
    return lax.ppermute(value, axis, [(i, i ^ bit) for i in range(lax.axis_size(axis))])


def fetch(value, step):
    size = lax.axis_size("fsdp")
    return lax.ppermute(value, "fsdp", [(i, (i - 2 * step) % size) for i in range(size)])


def after(value, *others):
    return lax.optimization_barrier((value,) + others)[0]


def phase(*values):
    return lax.optimization_barrier(values)


def local(hidden_in, gain_in, w_key, key_gain, partner):
    own_index = lax.axis_index("mp")
    teacher = partner[own_index]
    place = lax.axis_index("fsdp")
    lines = lax.axis_size("fsdp") // 2
    tok_rows, width = hidden_in.shape[1:]
    rows, features = w_key.shape[1:]
    head = key_gain.shape[1]

    far = lines // 2
    near = [step for step in range(1, lines) if step != far]
    order = [(0, 0), (0, 1)] + [(step, 0) for step in near]
    order += [(step, 1) for step in near[:-1]] + [(far, 0), (near[-1], 1), (far, 1)]
    place = place.astype(jnp.int32).reshape(1)
    own = w_key[0]

    same, other = {(0, 0): own}, {}
    for step in near:
        same[step, 0] = fetch(own, step)
    same[0, 1] = swap(own, "fsdp", 1)
    other[0, 0] = swap(own, "mp", 2)
    other[0, 1] = swap(same[0, 1], "mp", 2)
    same[far, 0] = fetch(after(own, same[near[0], 0]), far)
    flags = [teacher == own_index ^ 2, teacher == own_index ^ 1, partner[own_index ^ 1] == own_index]
    choice, across, offer = [jnp.where(flag, 0, 1).astype(jnp.int32).reshape(1) for flag in flags]
    place, choice, across, offer = phase(place, choice, across, offer)
    student = normed_input(place, hidden_in[0], gain_in.astype(jnp.float32), order, rows)
    gains_own = jnp.concatenate([gain_in, key_gain], axis=1)
    gains_beside = swap(gains_own, "mp", 2)
    student, gains_beside, other[0, 0], other[0, 1], *moved = phase(
        student, gains_beside, other[0, 0], other[0, 1], *[same[step, 0] for step in near]
    )
    gains_same = jnp.concatenate([gains_own, gains_beside], axis=0)
    gains_cross = swap(gains_same, "mp", 1)
    gains_teacher = jnp.where(
        choice == 0, gains_same[1:], jnp.where(across == 0, gains_cross[:1], gains_cross[1:])
    ).astype(jnp.float32)
    normed = normed_input(place, after(hidden_in[0], student), gains_teacher[:, :width], order, rows)

    for step, block in zip(near, moved):
        same[step, 0] = block
        other[step, 0] = swap(block, "mp", 2)
        same[step, 1] = swap(block, "fsdp", 1)
    same[far, 1] = fetch(after(same[0, 1], other[near[0], 0], same[near[0], 1]), far)

    arrived = phase(
        same[far, 0],
        normed,
        *[same[step, 1] for step in near],
        *[other[step, 0] for step in near],
    )
    same[far, 0], normed = arrived[:2]
    for i, step in enumerate(near):
        same[step, 1], other[step, 0] = arrived[2 + i], arrived[2 + len(near) + i]
    other[far, 0] = swap(same[far, 0], "mp", 2)
    for i, step in enumerate(near):
        other[step, 1] = swap(other[step, 0], "fsdp", 1) if i % 2 == 0 else swap(same[step, 1], "mp", 2)

    def cross(keys, *wait):
        return swap(pack(after(offer, *wait), [same[key] for key in keys], [other[key] for key in keys]), "mp", 1)

    first, second, third = order[: 2 + len(near)], order[2 + len(near) : -2], order[-2:]
    part_s = early_keys(choice, student, [[same[key] for key in first + second]], 0)
    other[far, 1] = swap(after(other[far, 0], part_s), "fsdp", 1)
    part_t = early_keys(choice, normed, [[other[key] for key in first], [cross(first)]], 0)
    crossed = cross(third, part_t)
    part_t = early_keys(choice, normed, [[other[key] for key in second], [cross(second)]], len(first) * rows, part_t)
    grad_keys, stats, keep_far, give_far = late_keys(
        choice,
        student,
        normed,
        part_s,
        part_t,
        key_gain.astype(jnp.float32),
        gains_teacher[:, width:],
        [same[key] for key in third],
        [[other[key] for key in third], [crossed]],
        rows,
        [order.index((far, pair)) for pair in range(2)],
    )

    wide = features // 2

    def grads(keys, dtype, *wait):
        return grad_blocks(after(grad_keys, *wait), student, rows, [order.index(key) for key in keys], dtype)

    sums = jnp.concatenate([stats[0], jnp.full((head,), jnp.sum(stats[1]))])
    bit, first_step = 2, None
    while bit < lax.axis_size("fsdp"):
        sums = sums + swap(sums, "fsdp", bit)
        first_step = sums if first_step is None else first_step
        bit *= 2
    given = [swap(give_far[:wide], "fsdp", 1), swap(after(give_far[wide:], first_step), "fsdp", 1)]
    pieces = grads([(step, 1) for step in near], jnp.bfloat16, given[0])
    keep = grads([(step, 0) for step in near], jnp.float32, pieces)
    ends = grads([(0, 0), (0, 1)], jnp.float32, keep)
    kept = [keep_far[i * wide : (i + 1) * wide] for i in range(2)] + [keep[i] for i in range(len(near))]
    arrived = []
    for at, step in enumerate([far, far] + near):
        if at >= 2:
            ready = given[0] if at == 2 else arrived[at - 3]
            given.append(swap(after(pieces[at - 2], ready), "fsdp", 1))
        mine, block = phase(kept[at], given[at])
        summed = (mine + block.astype(jnp.float32)).astype(jnp.bfloat16)
        arrived.append(fetch(after(summed, [summed, sums, *arrived][at]), -step))
    last = swap(after(ends[1].astype(jnp.bfloat16), given[2], arrived[1]), "fsdp", 1)
    sums = sums + swap(after(sums, given[-1]), "fsdp", 1)
    total = ends[0] + last.astype(jnp.float32) + jnp.concatenate(arrived[:2], axis=0).astype(jnp.float32)
    for block in arrived[2:]:
        total = total + block.astype(jnp.float32)

    tokens_all = tok_rows * lax.axis_size("fsdp")
    distill_loss = (sums[head] / (tokens_all * features)).reshape(1)
    return (total.T[None], sums[None, :head], distill_loss)


def norm_input(hidden, gain):
    values = hidden.astype(jnp.float32)
    scale = lax.rsqrt(jnp.mean(values * values, axis=-1, keepdims=True) + EPS)
    return (values * scale * gain.astype(jnp.float32)).astype(jnp.bfloat16)


def norm_keys(keys, gain):
    heads = keys.reshape(keys.shape[0], -1, gain.shape[0])
    inverse = lax.rsqrt(jnp.mean(heads * heads, axis=-1, keepdims=True) + EPS)
    return (heads, inverse, heads * inverse * gain.astype(jnp.float32))


def plain(hidden_in, gain_in, w_key, key_gain, partner):
    partner_index = partner[lax.axis_index("mp")]
    every = [lax.all_gather(array, "mp", axis=0, tiled=True) for array in (w_key, gain_in, key_gain)]
    teach_w, teach_gain, teach_key_gain = [
        lax.dynamic_index_in_dim(array, partner_index, 0, keepdims=False) for array in every
    ]
    normed_student = norm_input(hidden_in[0], gain_in[0])
    normed_teacher = norm_input(hidden_in[0], teach_gain)
    keys_student, keys_teacher = [
        jnp.dot(normed, lax.all_gather(weight, "fsdp", axis=0, tiled=True), preferred_element_type=jnp.float32)
        for normed, weight in ((normed_student, w_key[0]), (normed_teacher, teach_w))
    ]
    heads, inverse, out_student = norm_keys(keys_student, key_gain[0])
    differ = out_student - norm_keys(keys_teacher, teach_key_gain)[2]
    upstream = differ / w_key.shape[2]
    weighted = upstream * key_gain[0].astype(jnp.float32)
    inner = jnp.sum(weighted * heads, axis=-1, keepdims=True)
    grad_heads = weighted * inverse - heads * inverse * inverse * inverse * inner / heads.shape[-1]
    grad_keys = grad_heads.reshape(keys_student.shape).astype(jnp.bfloat16)
    grad_gain = jnp.sum(upstream * heads * inverse, axis=(0, 1))
    loss_total, gain_total = lax.psum((jnp.sum(differ * differ), grad_gain), "fsdp")
    tokens_all = hidden_in.shape[1] * lax.axis_size("fsdp")
    grad = lax.dot_general(
        normed_student, grad_keys, (((0,), (0,)), ((), ())), preferred_element_type=jnp.float32
    )
    grad_rows = lax.psum_scatter(grad, "fsdp", scatter_dimension=0, tiled=True)
    distill_loss = (loss_total / (tokens_all * w_key.shape[2])).reshape(1)
    return (grad_rows[None], gain_total[None], distill_loss)


def step(hidden_in, gain_in, w_key, key_gain, partner):
    body = plain if w_key.shape[1] % 128 else local
    return body(hidden_in, gain_in, w_key, key_gain, partner)


def solution(mesh):
    return jax.shard_map(
        step,
        mesh=mesh,
        in_specs=(P("mp", "fsdp", None), P("mp", None), P("mp", "fsdp", None), P("mp", None), P()),
        out_specs=(P("mp", "fsdp", None), P("mp", None), P("mp")),
        check_vma=False,
    )
```

```python
import functools

import jax
import jax.numpy as jnp
from jax import lax
from jax.experimental import pallas as pl
from jax.experimental.pallas import tpu as pltpu
from jax.sharding import PartitionSpec as P

EPS = 1e-06
NORM_TOKENS = 128
KEY_TOKENS = 256
VMEM_LIMIT = 16 * 1024 * 1024
SHORT = pl.CostEstimate(flops=1, bytes_accessed=1, transcendentals=0)
ANY = pl.BlockSpec(memory_space=pl.ANY)
SMEM = pl.BlockSpec(memory_space=pltpu.SMEM)


def norm_kernel(order, rows, place_ref, hidden_ref, gain_ref, out_ref):
    values = hidden_ref[...].astype(jnp.float32)
    scale = lax.rsqrt(jnp.sum(values * values, axis=-1, keepdims=True) / values.shape[1] + EPS)
    line, member = lax.div(place_ref[0], 2), lax.rem(place_ref[0], 2)
    for at, (step, pair) in enumerate(order):
        owner = lax.rem(line + step, len(order) // 2) * 2 + lax.rem(member + pair, 2)
        source = pl.ds(pl.multiple_of(owner * rows, 128), rows)
        scaled = hidden_ref[:, source].astype(jnp.float32) * scale * gain_ref[:, source]
        out_ref[:, at * rows : (at + 1) * rows] = scaled.astype(jnp.bfloat16)


def normed_input(place, hidden, gain, order, rows):
    tokens, width = hidden.shape
    block = pl.BlockSpec((NORM_TOKENS, width), lambda i: (i, 0))
    return pl.pallas_call(
        functools.partial(norm_kernel, order, rows),
        grid=(tokens // NORM_TOKENS,),
        in_specs=[SMEM, block, pl.BlockSpec((1, width), lambda i: (0, 0))],
        out_specs=block,
        out_shape=pltpu.HBM(hidden.shape, jnp.bfloat16),
        compiler_params=pltpu.CompilerParams(vmem_limit_bytes=VMEM_LIMIT),
        cost_estimate=SHORT,
        name="norm_input",
    )(place, in_hbm(hidden), gain)


def copy_blocks(sources, target, sems):
    copies, at = [], 0
    for i, source in enumerate(sources):
        rows = source.shape[0]
        copies.append(pltpu.make_async_copy(source, target.at[pl.ds(at, rows)], sems.at[i]))
        at += rows
    for copy in copies:
        copy.start()
    return copies


def load_weights(choice_ref, choices, target, sems):
    def load(sources):
        for copy in copy_blocks(sources, target, sems):
            copy.wait()

    if len(choices) == 1:
        load(choices[0])
    else:
        for i, sources in enumerate(choices):
            pl.when(choice_ref[0] == i)(functools.partial(load, sources))


def in_hbm(array):
    return pltpu.with_memory_space_constraint(array, pltpu.HBM)


def split(refs, counts):
    lists = []
    for count in counts:
        lists.append(refs[:count])
        refs = refs[count:]
    return lists, refs


def pack_kernel(counts, choice_ref, *refs):
    choices, (out_ref, sems) = split(refs, counts)
    load_weights(choice_ref, choices, out_ref, sems)


def pack(choice, *choices):
    rows, wide = sum(block.shape[0] for block in choices[0]), choices[0][0].shape[1]
    counts = [len(blocks) for blocks in choices]
    return pl.pallas_call(
        functools.partial(pack_kernel, counts),
        in_specs=[SMEM] + [ANY] * sum(counts),
        out_specs=pl.BlockSpec(memory_space=pltpu.VMEM),
        out_shape=jax.ShapeDtypeStruct((rows, wide), choices[0][0].dtype),
        scratch_shapes=[pltpu.SemaphoreType.DMA((max(counts),))],
        compiler_params=pltpu.CompilerParams(vmem_limit_bytes=VMEM_LIMIT),
        cost_estimate=SHORT,
        name="pack_blocks",
    )(choice, *[block for blocks in choices for block in blocks])


def early_kernel(counts, adds, choice_ref, normed_ref, *refs):
    choices, refs = split(refs, counts)
    before, (keys_ref, weights, sems) = refs[:-3], refs[-3:]

    @pl.when(pl.program_id(0) == 0)
    def _():
        load_weights(choice_ref, choices, weights, sems)

    keys = jnp.dot(normed_ref[...], weights[...], preferred_element_type=jnp.float32)
    keys_ref[...] = keys + before[0][...] if adds else keys


def early_keys(choice, normed, choices, first, before=None):
    depth, wide, tokens = sum(block.shape[0] for block in choices[0]), choices[0][0].shape[1], normed.shape[0]
    counts = [len(blocks) for blocks in choices]
    keys = pl.BlockSpec((KEY_TOKENS, wide), lambda i: (i, 0))
    before = [] if before is None else [before]
    return pl.pallas_call(
        functools.partial(early_kernel, counts, bool(before)),
        grid=(tokens // KEY_TOKENS,),
        in_specs=[SMEM, pl.BlockSpec((KEY_TOKENS, depth), lambda i: (i, first // depth))]
        + [ANY] * sum(counts)
        + [keys] * len(before),
        out_specs=keys,
        out_shape=jax.ShapeDtypeStruct((tokens, wide), jnp.float32),
        scratch_shapes=[pltpu.VMEM((depth, wide), jnp.bfloat16), pltpu.SemaphoreType.DMA((max(counts),))],
        compiler_params=pltpu.CompilerParams(vmem_limit_bytes=VMEM_LIMIT),
        cost_estimate=SHORT,
        name="early_keys",
    )(choice, in_hbm(normed), *[block for blocks in choices for block in blocks], *before)


def late_kernel(counts, choice_ref, student_ref, teacher_ref, part_s_ref, part_t_ref, gain_s_ref, gain_t_ref, *refs):
    (same, *choices), refs = split(refs, counts)
    give_of_ref, grad_ref, stats_ref, give_ref, w_s, w_t, sems_s, sems_t = refs
    step = pl.program_id(0)
    head, features = gain_s_ref.shape[1], part_s_ref.shape[1]

    @pl.when(step == 0)
    def _():
        own = copy_blocks(same, w_s, sems_s)
        load_weights(choice_ref, choices, w_t, sems_t)
        for copy in own:
            copy.wait()

    keys_s = part_s_ref[...] + jnp.dot(student_ref[...], w_s[...], preferred_element_type=jnp.float32)
    keys_t = part_t_ref[...] + jnp.dot(teacher_ref[...], w_t[...], preferred_element_type=jnp.float32)
    gain_s, gain_t = gain_s_ref[...], gain_t_ref[...]
    gain_sum, loss_sum = 0.0, 0.0
    tokens = pl.ds(pl.multiple_of(step * keys_s.shape[0], 256), keys_s.shape[0])
    for at in range(0, features, head):
        heads, taught = keys_s[:, at : at + head], keys_t[:, at : at + head]
        inverse = lax.rsqrt(jnp.mean(heads * heads, axis=-1, keepdims=True) + EPS)
        inverse_t = lax.rsqrt(jnp.mean(taught * taught, axis=-1, keepdims=True) + EPS)
        differ = heads * inverse * gain_s - taught * inverse_t * gain_t
        upstream = differ * (1.0 / features)
        weighted = upstream * gain_s
        inner = jnp.sum(weighted * heads, axis=-1, keepdims=True)
        grad = weighted * inverse - heads * (inverse * inverse * inverse * inner / head)
        grad_ref[tokens, at : at + head] = grad.astype(jnp.bfloat16)
        gain_sum = gain_sum + jnp.sum(upstream * heads * inverse, axis=0, keepdims=True)
        loss_sum = loss_sum + jnp.sum(differ * differ, axis=0, keepdims=True)
    stats = jnp.concatenate([gain_sum, loss_sum, jnp.zeros((6, head), jnp.float32)], axis=0)

    @pl.when(step == 0)
    def _():
        stats_ref[...] = stats

    @pl.when(step != 0)
    def _():
        stats_ref[...] += stats

    @pl.when(step == pl.num_programs(0) - 1)
    def _():
        give_ref[...] = lax.dot_general(
            grad_ref[...], give_of_ref[...], (((0,), (0,)), ((), ())), preferred_element_type=jnp.float32
        ).astype(give_ref.dtype)


def late_keys(choice, student, teacher, part_s, part_t, gain_s, gain_t, same, choices, rows, give):
    counts, (tokens, wide), head = [len(same)] + [len(blocks) for blocks in choices], part_s.shape, gain_s.shape[1]
    depth = sum(block.shape[0] for block in same)
    last = student.shape[1] // depth - 1
    token_block = pl.BlockSpec((KEY_TOKENS, depth), lambda i: (i, last))
    keys = pl.BlockSpec((KEY_TOKENS, wide), lambda i: (i, 0))
    gain = pl.BlockSpec((1, head), lambda i: (0, 0))
    outs = [
        jax.ShapeDtypeStruct((tokens, wide), jnp.bfloat16),
        jax.ShapeDtypeStruct((8, head), jnp.float32),
        jax.ShapeDtypeStruct((wide, rows), jnp.bfloat16),
    ]
    student, teacher = in_hbm(student), in_hbm(teacher)
    return pl.pallas_call(
        functools.partial(late_kernel, counts),
        grid=(tokens // KEY_TOKENS,),
        in_specs=[SMEM, token_block, token_block, keys, keys, gain, gain] + [ANY] * sum(counts)
        + [pl.BlockSpec((tokens, rows), lambda i: (0, give))],
        out_specs=[pl.BlockSpec(out.shape, lambda i: (0, 0)) for out in outs],
        out_shape=outs,
        scratch_shapes=[pltpu.VMEM((depth, wide), jnp.bfloat16)] * 2
        + [pltpu.SemaphoreType.DMA((count,)) for count in (counts[0], max(counts[1:]))],
        compiler_params=pltpu.CompilerParams(vmem_limit_bytes=VMEM_LIMIT),
        cost_estimate=SHORT,
        name="late_keys",
    )(
        choice,
        student,
        teacher,
        part_s,
        part_t,
        gain_s,
        gain_t,
        *same,
        *[block for blocks in choices for block in blocks],
        student,
    )


def grad_kernel(grad_ref, student_ref, out_ref):
    out_ref[0] = lax.dot_general(
        grad_ref[...], student_ref[...], (((0,), (0,)), ((), ())), preferred_element_type=jnp.float32
    ).astype(out_ref.dtype)


def grad_blocks(grad_keys, student, rows, blocks, dtype):
    (tokens, wide), count, first = grad_keys.shape, len(blocks), blocks[0]
    stride = blocks[1] - first if count > 1 else 1
    return pl.pallas_call(
        grad_kernel,
        grid=(count,),
        in_specs=[
            pl.BlockSpec((tokens, wide), lambda i: (0, 0)),
            pl.BlockSpec((tokens, rows), lambda i: (0, first + stride * i)),
        ],
        out_specs=pl.BlockSpec((1, wide, rows), lambda i: (i, 0, 0)),
        out_shape=jax.ShapeDtypeStruct((count, wide, rows), dtype),
        compiler_params=pltpu.CompilerParams(vmem_limit_bytes=VMEM_LIMIT),
        cost_estimate=SHORT,
        name="grad_blocks",
    )(grad_keys, in_hbm(student))


def swap(value, axis, bit):
    return lax.ppermute(value, axis, [(i, i ^ bit) for i in range(lax.axis_size(axis))])


def fetch(value, step):
    size = lax.axis_size("fsdp")
    return lax.ppermute(value, "fsdp", [(i, (i - 2 * step) % size) for i in range(size)])


def after(value, *others):
    return lax.optimization_barrier((value,) + others)[0]


def phase(*values):
    return lax.optimization_barrier(values)


def local(hidden_in, gain_in, w_key, key_gain, partner):
    own_index = lax.axis_index("mp")
    teacher = partner[own_index]
    place = lax.axis_index("fsdp")
    lines = lax.axis_size("fsdp") // 2
    tok_rows, width = hidden_in.shape[1:]
    rows, features = w_key.shape[1:]
    head = key_gain.shape[1]

    far = lines // 2
    near = [step for step in range(1, lines) if step != far]
    order = [(0, 0), (0, 1)] + [(step, 0) for step in near]
    order += [(step, 1) for step in near[:-1]] + [(far, 0), (near[-1], 1), (far, 1)]
    place = place.astype(jnp.int32).reshape(1)
    own = w_key[0]

    same, other = {(0, 0): own}, {}
    for step in near:
        same[step, 0] = fetch(own, step)
    same[0, 1] = swap(own, "fsdp", 1)
    other[0, 0] = swap(own, "mp", 2)
    other[0, 1] = swap(same[0, 1], "mp", 2)
    same[far, 0] = fetch(after(own, same[near[0], 0]), far)
    flags = [teacher == own_index ^ 2, teacher == own_index ^ 1, partner[own_index ^ 1] == own_index]
    choice, across, offer = [jnp.where(flag, 0, 1).astype(jnp.int32).reshape(1) for flag in flags]
    place, choice, across, offer = phase(place, choice, across, offer)
    student = normed_input(place, hidden_in[0], gain_in.astype(jnp.float32), order, rows)
    gains_own = jnp.concatenate([gain_in, key_gain], axis=1)
    gains_beside = swap(gains_own, "mp", 2)
    student, gains_beside, other[0, 0], other[0, 1], *moved = phase(
        student, gains_beside, other[0, 0], other[0, 1], *[same[step, 0] for step in near]
    )
    gains_same = jnp.concatenate([gains_own, gains_beside], axis=0)
    gains_cross = swap(gains_same, "mp", 1)
    gains_teacher = jnp.where(
        choice == 0, gains_same[1:], jnp.where(across == 0, gains_cross[:1], gains_cross[1:])
    ).astype(jnp.float32)
    normed = normed_input(place, after(hidden_in[0], student), gains_teacher[:, :width], order, rows)

    for step, block in zip(near, moved):
        same[step, 0] = block
        other[step, 0] = swap(block, "mp", 2)
        same[step, 1] = swap(block, "fsdp", 1)
    same[far, 1] = fetch(after(same[0, 1], other[near[0], 0], same[near[0], 1]), far)

    arrived = phase(
        same[far, 0],
        normed,
        *[same[step, 1] for step in near],
        *[other[step, 0] for step in near],
    )
    same[far, 0], normed = arrived[:2]
    for i, step in enumerate(near):
        same[step, 1], other[step, 0] = arrived[2 + i], arrived[2 + len(near) + i]
    other[far, 0] = swap(same[far, 0], "mp", 2)
    for i, step in enumerate(near):
        other[step, 1] = swap(other[step, 0], "fsdp", 1) if i % 2 == 0 else swap(same[step, 1], "mp", 2)

    def cross(keys, *wait):
        return swap(pack(after(offer, *wait), [same[key] for key in keys], [other[key] for key in keys]), "mp", 1)

    first, second, third = order[: 2 + len(near)], order[2 + len(near) : -2], order[-2:]
    part_s = early_keys(choice, student, [[same[key] for key in first + second]], 0)
    other[far, 1] = swap(after(other[far, 0], part_s), "fsdp", 1)
    part_t = early_keys(choice, normed, [[other[key] for key in first], [cross(first)]], 0)
    crossed = cross(third, part_t)
    part_t = early_keys(choice, normed, [[other[key] for key in second], [cross(second)]], len(first) * rows, part_t)
    grad_keys, sums, give_far = late_keys(
        choice,
        student,
        normed,
        part_s,
        part_t,
        key_gain.astype(jnp.float32),
        gains_teacher[:, width:],
        [same[key] for key in third],
        [[other[key] for key in third], [crossed]],
        rows,
        order.index((far, 1)),
    )

    wide = features // 2

    def grads(keys, dtype, *wait):
        return grad_blocks(after(grad_keys, *wait), student, rows, [order.index(key) for key in keys], dtype)

    keep_far = grads([(far, 0)], jnp.float32, give_far)
    halves = [slice(0, wide), slice(wide, features)]
    given = [swap(give_far[halves[0]], "fsdp", 1), swap(after(give_far[halves[1]], keep_far), "fsdp", 1)]
    bit = 2
    while bit < lax.axis_size("fsdp"):
        sums = sums + swap(sums, "fsdp", bit)
        bit *= 2
    pieces = grads([(step, 1) for step in near], jnp.bfloat16, given[0])
    keep = grads([(step, 0) for step in near], jnp.float32, pieces)
    ends = grads([(0, 0), (0, 1)], jnp.float32, keep)
    kept = [keep_far[0, half] for half in halves] + [keep[i] for i in range(len(near))]
    arrived = []
    for at, step in enumerate([far, far] + near):
        if at >= 2:
            given.append(swap(after(pieces[at - 2], [given[0], arrived[0]][at - 2]), "fsdp", 1))
        mine, block = phase(kept[at], given[at])
        summed = (mine + block.astype(jnp.float32)).astype(jnp.bfloat16)
        arrived.append(fetch(after(summed, [summed, sums, *arrived][at]), -step))
    last = swap(after(ends[1].astype(jnp.bfloat16), given[2], arrived[1]), "fsdp", 1)
    sums = sums + swap(after(sums, given[3]), "fsdp", 1)
    total = ends[0] + last.astype(jnp.float32) + jnp.concatenate(arrived[:2], axis=0).astype(jnp.float32)
    for block in arrived[2:]:
        total = total + block.astype(jnp.float32)

    tokens_all = tok_rows * lax.axis_size("fsdp")
    distill_loss = (jnp.sum(sums[1]) / (tokens_all * features)).reshape(1)
    return (total.T[None], sums[:1], distill_loss)


def norm_input(hidden, gain):
    values = hidden.astype(jnp.float32)
    scale = lax.rsqrt(jnp.mean(values * values, axis=-1, keepdims=True) + EPS)
    return (values * scale * gain.astype(jnp.float32)).astype(jnp.bfloat16)


def norm_keys(keys, gain):
    heads = keys.reshape(keys.shape[0], -1, gain.shape[0])
    inverse = lax.rsqrt(jnp.mean(heads * heads, axis=-1, keepdims=True) + EPS)
    return (heads, inverse, heads * inverse * gain.astype(jnp.float32))


def plain(hidden_in, gain_in, w_key, key_gain, partner):
    partner_index = partner[lax.axis_index("mp")]
    every = [lax.all_gather(array, "mp", axis=0, tiled=True) for array in (w_key, gain_in, key_gain)]
    teach_w, teach_gain, teach_key_gain = [
        lax.dynamic_index_in_dim(array, partner_index, 0, keepdims=False) for array in every
    ]
    normed_student = norm_input(hidden_in[0], gain_in[0])
    normed_teacher = norm_input(hidden_in[0], teach_gain)
    keys_student, keys_teacher = [
        jnp.dot(normed, lax.all_gather(weight, "fsdp", axis=0, tiled=True), preferred_element_type=jnp.float32)
        for normed, weight in ((normed_student, w_key[0]), (normed_teacher, teach_w))
    ]
    heads, inverse, out_student = norm_keys(keys_student, key_gain[0])
    differ = out_student - norm_keys(keys_teacher, teach_key_gain)[2]
    upstream = differ / w_key.shape[2]
    weighted = upstream * key_gain[0].astype(jnp.float32)
    inner = jnp.sum(weighted * heads, axis=-1, keepdims=True)
    grad_heads = weighted * inverse - heads * inverse * inverse * inverse * inner / heads.shape[-1]
    grad_keys = grad_heads.reshape(keys_student.shape).astype(jnp.bfloat16)
    grad_gain = jnp.sum(upstream * heads * inverse, axis=(0, 1))
    loss_total, gain_total = lax.psum((jnp.sum(differ * differ), grad_gain), "fsdp")
    tokens_all = hidden_in.shape[1] * lax.axis_size("fsdp")
    grad = lax.dot_general(
        normed_student, grad_keys, (((0,), (0,)), ((), ())), preferred_element_type=jnp.float32
    )
    grad_rows = lax.psum_scatter(grad, "fsdp", scatter_dimension=0, tiled=True)
    distill_loss = (loss_total / (tokens_all * w_key.shape[2])).reshape(1)
    return (grad_rows[None], gain_total[None], distill_loss)


def step(hidden_in, gain_in, w_key, key_gain, partner):
    body = plain if w_key.shape[1] % 128 else local
    return body(hidden_in, gain_in, w_key, key_gain, partner)


def solution(mesh):
    return jax.shard_map(
        step,
        mesh=mesh,
        in_specs=(P("mp", "fsdp", None), P("mp", None), P("mp", "fsdp", None), P("mp", None), P()),
        out_specs=(P("mp", "fsdp", None), P("mp", None), P("mp")),
        check_vma=False,
    )
```

```python
import functools

import jax
import jax.numpy as jnp
from jax import lax
from jax.experimental import pallas as pl
from jax.experimental.pallas import tpu as pltpu
from jax.sharding import PartitionSpec as P

EPS = 1e-06
NORM_TOKENS = 128
KEY_TOKENS = 256
VMEM_LIMIT = 16 * 1024 * 1024
SHORT = pl.CostEstimate(flops=1, bytes_accessed=1, transcendentals=0)
ANY = pl.BlockSpec(memory_space=pl.ANY)
SMEM = pl.BlockSpec(memory_space=pltpu.SMEM)


def norm_kernel(order, rows, place_ref, hidden_ref, gain_ref, out_ref):
    values = hidden_ref[...].astype(jnp.float32)
    scale = lax.rsqrt(jnp.sum(values * values, axis=-1, keepdims=True) / values.shape[1] + EPS)
    line, member = lax.div(place_ref[0], 2), lax.rem(place_ref[0], 2)
    for at, (step, pair) in enumerate(order):
        owner = lax.rem(line + step, len(order) // 2) * 2 + lax.rem(member + pair, 2)
        source = pl.ds(pl.multiple_of(owner * rows, 128), rows)
        scaled = hidden_ref[:, source].astype(jnp.float32) * scale * gain_ref[:, source]
        out_ref[:, at * rows : (at + 1) * rows] = scaled.astype(jnp.bfloat16)


def normed_input(place, hidden, gain, order, rows):
    tokens, width = hidden.shape
    block = pl.BlockSpec((NORM_TOKENS, width), lambda i: (i, 0))
    return pl.pallas_call(
        functools.partial(norm_kernel, order, rows),
        grid=(tokens // NORM_TOKENS,),
        in_specs=[SMEM, block, pl.BlockSpec((1, width), lambda i: (0, 0))],
        out_specs=block,
        out_shape=pltpu.HBM(hidden.shape, jnp.bfloat16),
        compiler_params=pltpu.CompilerParams(vmem_limit_bytes=VMEM_LIMIT),
        cost_estimate=SHORT,
        name="norm_input",
    )(place, in_hbm(hidden), gain)


def copy_blocks(sources, target, sems):
    copies, at = [], 0
    for i, source in enumerate(sources):
        rows = source.shape[0]
        copies.append(pltpu.make_async_copy(source, target.at[pl.ds(at, rows)], sems.at[i]))
        at += rows
    for copy in copies:
        copy.start()
    return copies


def load_weights(choice_ref, choices, target, sems):
    def load(sources):
        for copy in copy_blocks(sources, target, sems):
            copy.wait()

    if len(choices) == 1:
        load(choices[0])
    else:
        for i, sources in enumerate(choices):
            pl.when(choice_ref[0] == i)(functools.partial(load, sources))


def in_hbm(array):
    return pltpu.with_memory_space_constraint(array, pltpu.HBM)


def split(refs, counts):
    lists = []
    for count in counts:
        lists.append(refs[:count])
        refs = refs[count:]
    return lists, refs


def pack_kernel(counts, choice_ref, *refs):
    choices, (out_ref, sems) = split(refs, counts)
    load_weights(choice_ref, choices, out_ref, sems)


def pack(choice, *choices):
    rows, wide = sum(block.shape[0] for block in choices[0]), choices[0][0].shape[1]
    counts = [len(blocks) for blocks in choices]
    return pl.pallas_call(
        functools.partial(pack_kernel, counts),
        in_specs=[SMEM] + [ANY] * sum(counts),
        out_specs=pl.BlockSpec(memory_space=pltpu.VMEM),
        out_shape=jax.ShapeDtypeStruct((rows, wide), choices[0][0].dtype),
        scratch_shapes=[pltpu.SemaphoreType.DMA((max(counts),))],
        compiler_params=pltpu.CompilerParams(vmem_limit_bytes=VMEM_LIMIT),
        cost_estimate=SHORT,
        name="pack_blocks",
    )(choice, *[block for blocks in choices for block in blocks])


def early_kernel(counts, adds, choice_ref, normed_ref, *refs):
    choices, refs = split(refs, counts)
    before, (keys_ref, weights, sems) = refs[:-3], refs[-3:]

    @pl.when(pl.program_id(0) == 0)
    def _():
        load_weights(choice_ref, choices, weights, sems)

    keys = jnp.dot(normed_ref[...], weights[...], preferred_element_type=jnp.float32)
    keys_ref[...] = keys + before[0][...] if adds else keys


def early_keys(choice, normed, choices, first, before=None):
    depth, wide, tokens = sum(block.shape[0] for block in choices[0]), choices[0][0].shape[1], normed.shape[0]
    counts = [len(blocks) for blocks in choices]
    keys = pl.BlockSpec((KEY_TOKENS, wide), lambda i: (i, 0))
    before = [] if before is None else [before]
    return pl.pallas_call(
        functools.partial(early_kernel, counts, bool(before)),
        grid=(tokens // KEY_TOKENS,),
        in_specs=[SMEM, pl.BlockSpec((KEY_TOKENS, depth), lambda i: (i, first // depth))]
        + [ANY] * sum(counts)
        + [keys] * len(before),
        out_specs=keys,
        out_shape=jax.ShapeDtypeStruct((tokens, wide), jnp.float32),
        scratch_shapes=[pltpu.VMEM((depth, wide), jnp.bfloat16), pltpu.SemaphoreType.DMA((max(counts),))],
        compiler_params=pltpu.CompilerParams(vmem_limit_bytes=VMEM_LIMIT),
        cost_estimate=SHORT,
        name="early_keys",
    )(choice, in_hbm(normed), *[block for blocks in choices for block in blocks], *before)


def late_kernel(counts, choice_ref, student_ref, teacher_ref, part_s_ref, part_t_ref, gain_s_ref, gain_t_ref, *refs):
    (same, *choices), refs = split(refs, counts)
    give_of_ref, grad_ref, stats_ref, give_ref, w_s, w_t, sems_s, sems_t = refs
    step = pl.program_id(0)
    head, features = gain_s_ref.shape[1], part_s_ref.shape[1]

    @pl.when(step == 0)
    def _():
        own = copy_blocks(same, w_s, sems_s)
        load_weights(choice_ref, choices, w_t, sems_t)
        for copy in own:
            copy.wait()

    keys_s = part_s_ref[...] + jnp.dot(student_ref[...], w_s[...], preferred_element_type=jnp.float32)
    keys_t = part_t_ref[...] + jnp.dot(teacher_ref[...], w_t[...], preferred_element_type=jnp.float32)
    gain_s, gain_t = gain_s_ref[...], gain_t_ref[...]
    gain_sum, loss_sum = 0.0, 0.0
    tokens = pl.ds(pl.multiple_of(step * keys_s.shape[0], 256), keys_s.shape[0])
    for at in range(0, features, head):
        heads, taught = keys_s[:, at : at + head], keys_t[:, at : at + head]
        inverse = lax.rsqrt(jnp.mean(heads * heads, axis=-1, keepdims=True) + EPS)
        inverse_t = lax.rsqrt(jnp.mean(taught * taught, axis=-1, keepdims=True) + EPS)
        differ = heads * inverse * gain_s - taught * inverse_t * gain_t
        upstream = differ * (1.0 / features)
        weighted = upstream * gain_s
        inner = jnp.sum(weighted * heads, axis=-1, keepdims=True)
        grad = weighted * inverse - heads * (inverse * inverse * inverse * inner / head)
        grad_ref[tokens, at : at + head] = grad.astype(jnp.bfloat16)
        gain_sum = gain_sum + jnp.sum(upstream * heads * inverse, axis=0, keepdims=True)
        loss_sum = loss_sum + jnp.sum(differ * differ, axis=0, keepdims=True)
    stats = jnp.concatenate([gain_sum, loss_sum, jnp.zeros((6, head), jnp.float32)], axis=0)

    @pl.when(step == 0)
    def _():
        stats_ref[...] = stats

    @pl.when(step != 0)
    def _():
        stats_ref[...] += stats

    @pl.when(step == pl.num_programs(0) - 1)
    def _():
        give_ref[...] = lax.dot_general(
            grad_ref[...], give_of_ref[...], (((0,), (0,)), ((), ())), preferred_element_type=jnp.float32
        ).astype(give_ref.dtype)


def late_keys(choice, student, teacher, part_s, part_t, gain_s, gain_t, same, choices, rows, give):
    counts, (tokens, wide), head = [len(same)] + [len(blocks) for blocks in choices], part_s.shape, gain_s.shape[1]
    depth = sum(block.shape[0] for block in same)
    last = student.shape[1] // depth - 1
    token_block = pl.BlockSpec((KEY_TOKENS, depth), lambda i: (i, last))
    keys = pl.BlockSpec((KEY_TOKENS, wide), lambda i: (i, 0))
    gain = pl.BlockSpec((1, head), lambda i: (0, 0))
    outs = [
        jax.ShapeDtypeStruct((tokens, wide), jnp.bfloat16),
        jax.ShapeDtypeStruct((8, head), jnp.float32),
        jax.ShapeDtypeStruct((wide, rows), jnp.bfloat16),
    ]
    student, teacher = in_hbm(student), in_hbm(teacher)
    return pl.pallas_call(
        functools.partial(late_kernel, counts),
        grid=(tokens // KEY_TOKENS,),
        in_specs=[SMEM, token_block, token_block, keys, keys, gain, gain] + [ANY] * sum(counts)
        + [pl.BlockSpec((tokens, rows), lambda i: (0, give))],
        out_specs=[pl.BlockSpec(out.shape, lambda i: (0, 0)) for out in outs],
        out_shape=outs,
        scratch_shapes=[pltpu.VMEM((depth, wide), jnp.bfloat16)] * 2
        + [pltpu.SemaphoreType.DMA((count,)) for count in (counts[0], max(counts[1:]))],
        compiler_params=pltpu.CompilerParams(vmem_limit_bytes=VMEM_LIMIT),
        cost_estimate=SHORT,
        name="late_keys",
    )(
        choice,
        student,
        teacher,
        part_s,
        part_t,
        gain_s,
        gain_t,
        *same,
        *[block for blocks in choices for block in blocks],
        student,
    )


def grad_kernel(grad_ref, student_ref, out_ref):
    out_ref[0] = lax.dot_general(
        grad_ref[...], student_ref[...], (((0,), (0,)), ((), ())), preferred_element_type=jnp.float32
    ).astype(out_ref.dtype)


def grad_blocks(grad_keys, student, rows, blocks, dtype):
    (tokens, wide), count, first = grad_keys.shape, len(blocks), blocks[0]
    stride = blocks[1] - first if count > 1 else 1
    return pl.pallas_call(
        grad_kernel,
        grid=(count,),
        in_specs=[
            pl.BlockSpec((tokens, wide), lambda i: (0, 0)),
            pl.BlockSpec((tokens, rows), lambda i: (0, first + stride * i)),
        ],
        out_specs=pl.BlockSpec((1, wide, rows), lambda i: (i, 0, 0)),
        out_shape=jax.ShapeDtypeStruct((count, wide, rows), dtype),
        compiler_params=pltpu.CompilerParams(vmem_limit_bytes=VMEM_LIMIT),
        cost_estimate=SHORT,
        name="grad_blocks",
    )(grad_keys, in_hbm(student))


def finish_kernel(ends_ref, last_ref, far_ref, far_rest_ref, *refs):
    *near_refs, out_ref = refs
    far = jnp.concatenate([far_ref[...].astype(jnp.float32), far_rest_ref[...].astype(jnp.float32)], axis=0)
    total = ends_ref[0] + last_ref[...].astype(jnp.float32) + far
    for near_ref in near_refs:
        total = total + near_ref[...].astype(jnp.float32)
    out_ref[...] = total.T


def finish(ends, last, arrived):
    wide, rows = last.shape
    blocks = [pl.BlockSpec((array.shape[0], 128), lambda i: (0, i)) for array in (last, *arrived)]
    return pl.pallas_call(
        finish_kernel,
        grid=(rows // 128,),
        in_specs=[pl.BlockSpec((1, wide, 128), lambda i: (0, 0, i))] + blocks,
        out_specs=pl.BlockSpec((128, wide), lambda i: (i, 0)),
        out_shape=jax.ShapeDtypeStruct((rows, wide), jnp.float32),
        compiler_params=pltpu.CompilerParams(vmem_limit_bytes=VMEM_LIMIT),
        cost_estimate=SHORT,
        name="finish",
    )(ends, last, *arrived)


def swap(value, axis, bit):
    return lax.ppermute(value, axis, [(i, i ^ bit) for i in range(lax.axis_size(axis))])


def fetch(value, step):
    size = lax.axis_size("fsdp")
    return lax.ppermute(value, "fsdp", [(i, (i - 2 * step) % size) for i in range(size)])


def after(value, *others):
    return lax.optimization_barrier((value,) + others)[0]


def phase(*values):
    return lax.optimization_barrier(values)


def local(hidden_in, gain_in, w_key, key_gain, partner):
    own_index = lax.axis_index("mp")
    teacher = partner[own_index]
    place = lax.axis_index("fsdp")
    lines = lax.axis_size("fsdp") // 2
    tok_rows, width = hidden_in.shape[1:]
    rows, features = w_key.shape[1:]
    head = key_gain.shape[1]

    far = lines // 2
    near = [step for step in range(1, lines) if step != far]
    order = [(0, 0), (0, 1)] + [(step, 0) for step in near]
    order += [(step, 1) for step in near[:-1]] + [(far, 0), (near[-1], 1), (far, 1)]
    place = place.astype(jnp.int32).reshape(1)
    own = w_key[0]

    same, other = {(0, 0): own}, {}
    for step in near:
        same[step, 0] = fetch(own, step)
    same[0, 1] = swap(own, "fsdp", 1)
    other[0, 0] = swap(own, "mp", 2)
    other[0, 1] = swap(same[0, 1], "mp", 2)
    same[far, 0] = fetch(after(own, same[near[0], 0]), far)
    flags = [teacher == own_index ^ 2, teacher == own_index ^ 1, partner[own_index ^ 1] == own_index]
    choice, across, offer = [jnp.where(flag, 0, 1).astype(jnp.int32).reshape(1) for flag in flags]
    place, choice, across, offer = phase(place, choice, across, offer)
    student = normed_input(place, hidden_in[0], gain_in.astype(jnp.float32), order, rows)
    gains_own = jnp.concatenate([gain_in, key_gain], axis=1)
    gains_beside = swap(gains_own, "mp", 2)
    student, gains_beside, other[0, 0], other[0, 1], *moved = phase(
        student, gains_beside, other[0, 0], other[0, 1], *[same[step, 0] for step in near]
    )
    gains_same = jnp.concatenate([gains_own, gains_beside], axis=0)
    gains_cross = swap(gains_same, "mp", 1)
    gains_teacher = jnp.where(
        choice == 0, gains_same[1:], jnp.where(across == 0, gains_cross[:1], gains_cross[1:])
    ).astype(jnp.float32)
    normed = normed_input(place, after(hidden_in[0], student), gains_teacher[:, :width], order, rows)

    for step, block in zip(near, moved):
        same[step, 0] = block
        other[step, 0] = swap(block, "mp", 2)
        same[step, 1] = swap(block, "fsdp", 1)
    same[far, 1] = fetch(after(same[0, 1], other[near[0], 0], same[near[0], 1]), far)

    arrived = phase(
        same[far, 0],
        normed,
        *[same[step, 1] for step in near],
        *[other[step, 0] for step in near],
    )
    same[far, 0], normed = arrived[:2]
    for i, step in enumerate(near):
        same[step, 1], other[step, 0] = arrived[2 + i], arrived[2 + len(near) + i]
    other[far, 0] = swap(same[far, 0], "mp", 2)
    for i, step in enumerate(near):
        other[step, 1] = swap(other[step, 0], "fsdp", 1) if i % 2 == 0 else swap(same[step, 1], "mp", 2)

    def cross(keys, *wait):
        return swap(pack(after(offer, *wait), [same[key] for key in keys], [other[key] for key in keys]), "mp", 1)

    first, second, third = order[: 2 + len(near)], order[2 + len(near) : -2], order[-2:]
    part_s = early_keys(choice, student, [[same[key] for key in first + second]], 0)
    other[far, 1] = swap(after(other[far, 0], part_s), "fsdp", 1)
    part_t = early_keys(choice, normed, [[other[key] for key in first], [cross(first)]], 0)
    crossed = cross(third, part_t)
    part_t = early_keys(choice, normed, [[other[key] for key in second], [cross(second)]], len(first) * rows, part_t)
    grad_keys, sums, give_far = late_keys(
        choice,
        student,
        normed,
        part_s,
        part_t,
        key_gain.astype(jnp.float32),
        gains_teacher[:, width:],
        [same[key] for key in third],
        [[other[key] for key in third], [crossed]],
        rows,
        order.index((far, 1)),
    )


    def grads(keys, dtype, *wait):
        return grad_blocks(after(grad_keys, *wait), student, rows, [order.index(key) for key in keys], dtype)

    halves = [slice(0, features // 4), slice(features // 4, features)]
    given = [swap(give_far[halves[0]], "fsdp", 1)]
    steps, bit = [], 2
    while bit < lax.axis_size("fsdp"):
        sums = sums + swap(sums, "fsdp", bit)
        steps.append(sums)
        bit *= 2
    keep_far = grads([(far, 0)], jnp.float32, steps[0])
    given.append(swap(after(give_far[halves[1]], keep_far), "fsdp", 1))
    pieces = grads([(step, 1) for step in near], jnp.bfloat16, given[0])
    keep = grads([(step, 0) for step in near], jnp.float32, pieces)
    ends = grads([(0, 0), (0, 1)], jnp.float32, keep)
    kept = [keep_far[0, half] for half in halves] + [keep[i] for i in range(len(near))]
    arrived = []
    for at, step in enumerate([far, far] + near):
        if at >= 2:
            given.append(swap(after(pieces[at - 2], [given[0], arrived[0]][at - 2]), "fsdp", 1))
        mine, block = phase(kept[at], given[at])
        summed = (mine + block.astype(jnp.float32)).astype(jnp.bfloat16)
        arrived.append(fetch(after(summed, [summed, sums, *arrived][at]), -step))
    last = swap(after(ends[1].astype(jnp.bfloat16), given[2], arrived[1]), "fsdp", 1)
    sums = sums + swap(after(sums, given[3]), "fsdp", 1)
    total = finish(ends, last, arrived)

    tokens_all = tok_rows * lax.axis_size("fsdp")
    distill_loss = (jnp.sum(sums[1]) / (tokens_all * features)).reshape(1)
    return (total[None], sums[:1], distill_loss)


def norm_input(hidden, gain):
    values = hidden.astype(jnp.float32)
    scale = lax.rsqrt(jnp.mean(values * values, axis=-1, keepdims=True) + EPS)
    return (values * scale * gain.astype(jnp.float32)).astype(jnp.bfloat16)


def norm_keys(keys, gain):
    heads = keys.reshape(keys.shape[0], -1, gain.shape[0])
    inverse = lax.rsqrt(jnp.mean(heads * heads, axis=-1, keepdims=True) + EPS)
    return (heads, inverse, heads * inverse * gain.astype(jnp.float32))


def plain(hidden_in, gain_in, w_key, key_gain, partner):
    partner_index = partner[lax.axis_index("mp")]
    every = [lax.all_gather(array, "mp", axis=0, tiled=True) for array in (w_key, gain_in, key_gain)]
    teach_w, teach_gain, teach_key_gain = [
        lax.dynamic_index_in_dim(array, partner_index, 0, keepdims=False) for array in every
    ]
    normed_student = norm_input(hidden_in[0], gain_in[0])
    normed_teacher = norm_input(hidden_in[0], teach_gain)
    keys_student, keys_teacher = [
        jnp.dot(normed, lax.all_gather(weight, "fsdp", axis=0, tiled=True), preferred_element_type=jnp.float32)
        for normed, weight in ((normed_student, w_key[0]), (normed_teacher, teach_w))
    ]
    heads, inverse, out_student = norm_keys(keys_student, key_gain[0])
    differ = out_student - norm_keys(keys_teacher, teach_key_gain)[2]
    upstream = differ / w_key.shape[2]
    weighted = upstream * key_gain[0].astype(jnp.float32)
    inner = jnp.sum(weighted * heads, axis=-1, keepdims=True)
    grad_heads = weighted * inverse - heads * inverse * inverse * inverse * inner / heads.shape[-1]
    grad_keys = grad_heads.reshape(keys_student.shape).astype(jnp.bfloat16)
    grad_gain = jnp.sum(upstream * heads * inverse, axis=(0, 1))
    loss_total, gain_total = lax.psum((jnp.sum(differ * differ), grad_gain), "fsdp")
    tokens_all = hidden_in.shape[1] * lax.axis_size("fsdp")
    grad = lax.dot_general(
        normed_student, grad_keys, (((0,), (0,)), ((), ())), preferred_element_type=jnp.float32
    )
    grad_rows = lax.psum_scatter(grad, "fsdp", scatter_dimension=0, tiled=True)
    distill_loss = (loss_total / (tokens_all * w_key.shape[2])).reshape(1)
    return (grad_rows[None], gain_total[None], distill_loss)


def step(hidden_in, gain_in, w_key, key_gain, partner):
    body = plain if w_key.shape[1] % 128 else local
    return body(hidden_in, gain_in, w_key, key_gain, partner)


def solution(mesh):
    return jax.shard_map(
        step,
        mesh=mesh,
        in_specs=(P("mp", "fsdp", None), P("mp", None), P("mp", "fsdp", None), P("mp", None), P()),
        out_specs=(P("mp", "fsdp", None), P("mp", None), P("mp")),
        check_vma=False,
    )
```

```python
import functools

import jax
import jax.numpy as jnp
from jax import lax
from jax.experimental import pallas as pl
from jax.experimental.pallas import tpu as pltpu
from jax.sharding import PartitionSpec as P

EPS = 1e-06
NORM_TOKENS = 128
KEY_TOKENS = 256
VMEM_LIMIT = 24 * 1024 * 1024
SHORT = pl.CostEstimate(flops=1, bytes_accessed=1, transcendentals=0)
ANY = pl.BlockSpec(memory_space=pl.ANY)
SMEM = pl.BlockSpec(memory_space=pltpu.SMEM)


def norm_kernel(order, rows, place_ref, hidden_ref, gain_ref, out_ref):
    values = hidden_ref[...].astype(jnp.float32)
    scale = lax.rsqrt(jnp.sum(values * values, axis=-1, keepdims=True) / values.shape[1] + EPS)
    line, member = lax.div(place_ref[0], 2), lax.rem(place_ref[0], 2)
    for at, (step, pair) in enumerate(order):
        owner = lax.rem(line + step, len(order) // 2) * 2 + lax.rem(member + pair, 2)
        source = pl.ds(pl.multiple_of(owner * rows, 128), rows)
        scaled = hidden_ref[:, source].astype(jnp.float32) * scale * gain_ref[:, source]
        out_ref[:, at * rows : (at + 1) * rows] = scaled.astype(jnp.bfloat16)


def normed_input(place, hidden, gain, order, rows):
    tokens, width = hidden.shape
    block = pl.BlockSpec((NORM_TOKENS, width), lambda i: (i, 0))
    return pl.pallas_call(
        functools.partial(norm_kernel, order, rows),
        grid=(tokens // NORM_TOKENS,),
        in_specs=[SMEM, block, pl.BlockSpec((1, width), lambda i: (0, 0))],
        out_specs=block,
        out_shape=pltpu.HBM(hidden.shape, jnp.bfloat16),
        compiler_params=pltpu.CompilerParams(vmem_limit_bytes=VMEM_LIMIT),
        cost_estimate=SHORT,
        name="norm_input",
    )(place, in_hbm(hidden), gain)


def copy_blocks(sources, target, sems):
    copies, at = [], 0
    for i, source in enumerate(sources):
        rows = source.shape[0]
        copies.append(pltpu.make_async_copy(source, target.at[pl.ds(at, rows)], sems.at[i]))
        at += rows
    for copy in copies:
        copy.start()
    return copies


def load_weights(choice_ref, choices, target, sems):
    def load(sources):
        for copy in copy_blocks(sources, target, sems):
            copy.wait()

    if len(choices) == 1:
        load(choices[0])
    else:
        for i, sources in enumerate(choices):
            pl.when(choice_ref[0] == i)(functools.partial(load, sources))


def in_hbm(array):
    return pltpu.with_memory_space_constraint(array, pltpu.HBM)


def split(refs, counts):
    lists = []
    for count in counts:
        lists.append(refs[:count])
        refs = refs[count:]
    return lists, refs


def pack_kernel(counts, choice_ref, *refs):
    choices, (out_ref, sems) = split(refs, counts)
    load_weights(choice_ref, choices, out_ref, sems)


def pack(choice, *choices):
    rows, wide = sum(block.shape[0] for block in choices[0]), choices[0][0].shape[1]
    counts = [len(blocks) for blocks in choices]
    return pl.pallas_call(
        functools.partial(pack_kernel, counts),
        in_specs=[SMEM] + [ANY] * sum(counts),
        out_specs=pl.BlockSpec(memory_space=pltpu.VMEM),
        out_shape=jax.ShapeDtypeStruct((rows, wide), choices[0][0].dtype),
        scratch_shapes=[pltpu.SemaphoreType.DMA((max(counts),))],
        compiler_params=pltpu.CompilerParams(vmem_limit_bytes=VMEM_LIMIT),
        cost_estimate=SHORT,
        name="pack_blocks",
    )(choice, *[block for blocks in choices for block in blocks])


def early_kernel(counts, adds, choice_ref, normed_ref, *refs):
    choices, refs = split(refs, counts)
    before, (keys_ref, weights, sems) = refs[:-3], refs[-3:]

    @pl.when(pl.program_id(0) == 0)
    def _():
        load_weights(choice_ref, choices, weights, sems)

    keys = jnp.dot(normed_ref[...], weights[...], preferred_element_type=jnp.float32)
    keys_ref[...] = keys + before[0][...] if adds else keys


def early_keys(choice, normed, choices, first, before=None):
    depth, wide, tokens = sum(block.shape[0] for block in choices[0]), choices[0][0].shape[1], normed.shape[0]
    counts = [len(blocks) for blocks in choices]
    keys = pl.BlockSpec((KEY_TOKENS, wide), lambda i: (i, 0))
    before = [] if before is None else [before]
    return pl.pallas_call(
        functools.partial(early_kernel, counts, bool(before)),
        grid=(tokens // KEY_TOKENS,),
        in_specs=[SMEM, pl.BlockSpec((KEY_TOKENS, depth), lambda i: (i, first // depth))]
        + [ANY] * sum(counts)
        + [keys] * len(before),
        out_specs=keys,
        out_shape=jax.ShapeDtypeStruct((tokens, wide), jnp.float32),
        scratch_shapes=[pltpu.VMEM((depth, wide), jnp.bfloat16), pltpu.SemaphoreType.DMA((max(counts),))],
        compiler_params=pltpu.CompilerParams(vmem_limit_bytes=VMEM_LIMIT),
        cost_estimate=SHORT,
        name="early_keys",
    )(choice, in_hbm(normed), *[block for blocks in choices for block in blocks], *before)


def late_kernel(counts, choice_ref, student_ref, teacher_ref, part_s_ref, part_t_ref, gain_s_ref, gain_t_ref, *refs):
    (same, *choices), refs = split(refs, counts)
    keep_of_ref, give_of_ref, grad_ref, stats_ref, keep_ref, give_ref, w_s, w_t, sems_s, sems_t = refs
    step = pl.program_id(0)
    head, features = gain_s_ref.shape[1], part_s_ref.shape[1]

    @pl.when(step == 0)
    def _():
        own = copy_blocks(same, w_s, sems_s)
        load_weights(choice_ref, choices, w_t, sems_t)
        for copy in own:
            copy.wait()

    keys_s = part_s_ref[...] + jnp.dot(student_ref[...], w_s[...], preferred_element_type=jnp.float32)
    keys_t = part_t_ref[...] + jnp.dot(teacher_ref[...], w_t[...], preferred_element_type=jnp.float32)
    gain_s, gain_t = gain_s_ref[...], gain_t_ref[...]
    gain_sum, loss_sum = 0.0, 0.0
    tokens = pl.ds(pl.multiple_of(step * keys_s.shape[0], 256), keys_s.shape[0])
    for at in range(0, features, head):
        heads, taught = keys_s[:, at : at + head], keys_t[:, at : at + head]
        inverse = lax.rsqrt(jnp.mean(heads * heads, axis=-1, keepdims=True) + EPS)
        inverse_t = lax.rsqrt(jnp.mean(taught * taught, axis=-1, keepdims=True) + EPS)
        differ = heads * inverse * gain_s - taught * inverse_t * gain_t
        upstream = differ * (1.0 / features)
        weighted = upstream * gain_s
        inner = jnp.sum(weighted * heads, axis=-1, keepdims=True)
        grad = weighted * inverse - heads * (inverse * inverse * inverse * inner / head)
        grad_ref[tokens, at : at + head] = grad.astype(jnp.bfloat16)
        gain_sum = gain_sum + jnp.sum(upstream * heads * inverse, axis=0, keepdims=True)
        loss_sum = loss_sum + jnp.sum(differ * differ, axis=0, keepdims=True)
    loss_sum = jnp.broadcast_to(jnp.sum(loss_sum, axis=1, keepdims=True), gain_sum.shape)
    stats = jnp.concatenate([gain_sum, loss_sum], axis=1)

    @pl.when(step == 0)
    def _():
        stats_ref[...] = stats

    @pl.when(step != 0)
    def _():
        stats_ref[...] += stats

    @pl.when(step == pl.num_programs(0) - 1)
    def _():
        for block_ref, out_ref in ((give_of_ref, give_ref), (keep_of_ref, keep_ref)):
            out_ref[...] = lax.dot_general(
                grad_ref[...], block_ref[...], (((0,), (0,)), ((), ())), preferred_element_type=jnp.float32
            ).astype(out_ref.dtype)


def late_keys(choice, student, teacher, part_s, part_t, gain_s, gain_t, same, choices, rows, far):
    counts, (tokens, wide), head = [len(same)] + [len(blocks) for blocks in choices], part_s.shape, gain_s.shape[1]
    depth = sum(block.shape[0] for block in same)
    last = student.shape[1] // depth - 1
    token_block = pl.BlockSpec((KEY_TOKENS, depth), lambda i: (i, last))
    keys = pl.BlockSpec((KEY_TOKENS, wide), lambda i: (i, 0))
    gain = pl.BlockSpec((1, head), lambda i: (0, 0))
    far_blocks = [pl.BlockSpec((tokens, rows), lambda i, at=at: (0, at)) for at in far]
    outs = [
        jax.ShapeDtypeStruct((tokens, wide), jnp.bfloat16),
        jax.ShapeDtypeStruct((1, 2 * head), jnp.float32),
        jax.ShapeDtypeStruct((wide, rows), jnp.float32),
        jax.ShapeDtypeStruct((wide, rows), jnp.bfloat16),
    ]
    student, teacher = in_hbm(student), in_hbm(teacher)
    return pl.pallas_call(
        functools.partial(late_kernel, counts),
        grid=(tokens // KEY_TOKENS,),
        in_specs=[SMEM, token_block, token_block, keys, keys, gain, gain] + [ANY] * sum(counts) + far_blocks,
        out_specs=[pl.BlockSpec(out.shape, lambda i: (0, 0)) for out in outs],
        out_shape=outs,
        scratch_shapes=[pltpu.VMEM((depth, wide), jnp.bfloat16)] * 2
        + [pltpu.SemaphoreType.DMA((count,)) for count in (counts[0], max(counts[1:]))],
        compiler_params=pltpu.CompilerParams(vmem_limit_bytes=VMEM_LIMIT),
        cost_estimate=SHORT,
        name="late_keys",
    )(
        choice,
        student,
        teacher,
        part_s,
        part_t,
        gain_s,
        gain_t,
        *same,
        *[block for blocks in choices for block in blocks],
        student,
        student,
    )


def grad_kernel(grad_ref, student_ref, out_ref):
    out_ref[0] = lax.dot_general(
        grad_ref[...], student_ref[...], (((0,), (0,)), ((), ())), preferred_element_type=jnp.float32
    ).astype(out_ref.dtype)


def grad_blocks(grad_keys, student, rows, blocks, dtype):
    (tokens, wide), count, first = grad_keys.shape, len(blocks), blocks[0]
    stride = blocks[1] - first if count > 1 else 1
    return pl.pallas_call(
        grad_kernel,
        grid=(count,),
        in_specs=[
            pl.BlockSpec((tokens, wide), lambda i: (0, 0)),
            pl.BlockSpec((tokens, rows), lambda i: (0, first + stride * i)),
        ],
        out_specs=pl.BlockSpec((1, wide, rows), lambda i: (i, 0, 0)),
        out_shape=jax.ShapeDtypeStruct((count, wide, rows), dtype),
        compiler_params=pltpu.CompilerParams(vmem_limit_bytes=VMEM_LIMIT),
        cost_estimate=SHORT,
        name="grad_blocks",
    )(grad_keys, in_hbm(student))


def swap(value, axis, bit):
    return lax.ppermute(value, axis, [(i, i ^ bit) for i in range(lax.axis_size(axis))])


def fetch(value, step):
    size = lax.axis_size("fsdp")
    return lax.ppermute(value, "fsdp", [(i, (i - 2 * step) % size) for i in range(size)])


def after(value, *others):
    return lax.optimization_barrier((value,) + others)[0]


def phase(*values):
    return lax.optimization_barrier(values)


def local(hidden_in, gain_in, w_key, key_gain, partner):
    own_index = lax.axis_index("mp")
    teacher = partner[own_index]
    place = lax.axis_index("fsdp")
    lines = lax.axis_size("fsdp") // 2
    tok_rows, width = hidden_in.shape[1:]
    rows, features = w_key.shape[1:]
    head = key_gain.shape[1]

    far = lines // 2
    near = [step for step in range(1, lines) if step != far]
    order = [(0, 0), (0, 1)] + [(step, 0) for step in near]
    order += [(step, 1) for step in near[:-1]] + [(far, 0), (near[-1], 1), (far, 1)]
    place = place.astype(jnp.int32).reshape(1)
    own = w_key[0]

    same, other = {(0, 0): own}, {}
    for step in near:
        same[step, 0] = fetch(own, step)
    same[0, 1] = swap(own, "fsdp", 1)
    other[0, 0] = swap(own, "mp", 2)
    other[0, 1] = swap(same[0, 1], "mp", 2)
    same[far, 0] = fetch(after(own, same[near[0], 0]), far)
    flags = [teacher == own_index ^ 2, teacher == own_index ^ 1, partner[own_index ^ 1] == own_index]
    choice, across, offer = [jnp.where(flag, 0, 1).astype(jnp.int32).reshape(1) for flag in flags]
    place, choice, across, offer = phase(place, choice, across, offer)
    student = normed_input(place, hidden_in[0], gain_in.astype(jnp.float32), order, rows)
    gains_own = jnp.concatenate([gain_in, key_gain], axis=1)
    gains_beside = swap(gains_own, "mp", 2)
    student, gains_beside, other[0, 0], other[0, 1], *moved = phase(
        student, gains_beside, other[0, 0], other[0, 1], *[same[step, 0] for step in near]
    )
    gains_same = jnp.concatenate([gains_own, gains_beside], axis=0)
    gains_cross = swap(gains_same, "mp", 1)
    gains_teacher = jnp.where(
        choice == 0, gains_same[1:], jnp.where(across == 0, gains_cross[:1], gains_cross[1:])
    ).astype(jnp.float32)
    normed = normed_input(place, after(hidden_in[0], student), gains_teacher[:, :width], order, rows)

    for step, block in zip(near, moved):
        same[step, 0] = block
        other[step, 0] = swap(block, "mp", 2)
        same[step, 1] = swap(block, "fsdp", 1)
    same[far, 1] = fetch(after(same[0, 1], other[near[0], 0], same[near[0], 1]), far)

    arrived = phase(
        same[far, 0],
        normed,
        *[same[step, 1] for step in near],
        *[other[step, 0] for step in near],
    )
    same[far, 0], normed = arrived[:2]
    for i, step in enumerate(near):
        same[step, 1], other[step, 0] = arrived[2 + i], arrived[2 + len(near) + i]
    other[far, 0] = swap(same[far, 0], "mp", 2)
    for i, step in enumerate(near):
        other[step, 1] = swap(other[step, 0], "fsdp", 1) if i % 2 == 0 else swap(same[step, 1], "mp", 2)

    def cross(keys, *wait):
        return swap(pack(after(offer, *wait), [same[key] for key in keys], [other[key] for key in keys]), "mp", 1)

    first, second, third = order[: 2 + len(near)], order[2 + len(near) : -2], order[-2:]
    part_s = early_keys(choice, student, [[same[key] for key in first + second]], 0)
    other[far, 1] = swap(after(other[far, 0], part_s), "fsdp", 1)
    part_t = early_keys(choice, normed, [[other[key] for key in first], [cross(first)]], 0)
    crossed = cross(third, part_t)
    part_t = early_keys(choice, normed, [[other[key] for key in second], [cross(second)]], len(first) * rows, part_t)
    grad_keys, stats, keep_far, give_far = late_keys(
        choice,
        student,
        normed,
        part_s,
        part_t,
        key_gain.astype(jnp.float32),
        gains_teacher[:, width:],
        [same[key] for key in third],
        [[other[key] for key in third], [crossed]],
        rows,
        [order.index((far, pair)) for pair in range(2)],
    )

    wide = features // 2

    def grads(keys, dtype, *wait):
        return grad_blocks(after(grad_keys, *wait), student, rows, [order.index(key) for key in keys], dtype)

    sums, bit, first_step = stats[0], 2, None
    while bit < lax.axis_size("fsdp"):
        sums = sums + swap(sums, "fsdp", bit)
        first_step = sums if first_step is None else first_step
        bit *= 2
    given = [swap(give_far[:wide], "fsdp", 1), swap(after(give_far[wide:], first_step), "fsdp", 1)]
    pieces = grads([(step, 1) for step in near], jnp.bfloat16, given[0])
    keep = grads([(step, 0) for step in near], jnp.float32, pieces)
    ends = grads([(0, 0), (0, 1)], jnp.float32, keep)
    kept = [keep_far[i * wide : (i + 1) * wide] for i in range(2)] + [keep[i] for i in range(len(near))]
    arrived = []
    for at, step in enumerate([far, far] + near):
        if at >= 2:
            ready = given[0] if at == 2 else arrived[at - 3]
            given.append(swap(after(pieces[at - 2], ready), "fsdp", 1))
        mine, block = phase(kept[at], given[at])
        summed = (mine + block.astype(jnp.float32)).astype(jnp.bfloat16)
        arrived.append(fetch(after(summed, [summed, sums, *arrived][at]), -step))
    last = swap(after(ends[1].astype(jnp.bfloat16), given[2], arrived[1]), "fsdp", 1)
    sums = sums + swap(after(sums, given[-1]), "fsdp", 1)
    total = ends[0] + last.astype(jnp.float32) + jnp.concatenate(arrived[:2], axis=0).astype(jnp.float32)
    for block in arrived[2:]:
        total = total + block.astype(jnp.float32)

    tokens_all = tok_rows * lax.axis_size("fsdp")
    distill_loss = (sums[head] / (tokens_all * features)).reshape(1)
    return (total.T[None], sums[None, :head], distill_loss)


def norm_input(hidden, gain):
    values = hidden.astype(jnp.float32)
    scale = lax.rsqrt(jnp.mean(values * values, axis=-1, keepdims=True) + EPS)
    return (values * scale * gain.astype(jnp.float32)).astype(jnp.bfloat16)


def norm_keys(keys, gain):
    heads = keys.reshape(keys.shape[0], -1, gain.shape[0])
    inverse = lax.rsqrt(jnp.mean(heads * heads, axis=-1, keepdims=True) + EPS)
    return (heads, inverse, heads * inverse * gain.astype(jnp.float32))


def plain(hidden_in, gain_in, w_key, key_gain, partner):
    partner_index = partner[lax.axis_index("mp")]
    every = [lax.all_gather(array, "mp", axis=0, tiled=True) for array in (w_key, gain_in, key_gain)]
    teach_w, teach_gain, teach_key_gain = [
        lax.dynamic_index_in_dim(array, partner_index, 0, keepdims=False) for array in every
    ]
    normed_student = norm_input(hidden_in[0], gain_in[0])
    normed_teacher = norm_input(hidden_in[0], teach_gain)
    keys_student, keys_teacher = [
        jnp.dot(normed, lax.all_gather(weight, "fsdp", axis=0, tiled=True), preferred_element_type=jnp.float32)
        for normed, weight in ((normed_student, w_key[0]), (normed_teacher, teach_w))
    ]
    heads, inverse, out_student = norm_keys(keys_student, key_gain[0])
    differ = out_student - norm_keys(keys_teacher, teach_key_gain)[2]
    upstream = differ / w_key.shape[2]
    weighted = upstream * key_gain[0].astype(jnp.float32)
    inner = jnp.sum(weighted * heads, axis=-1, keepdims=True)
    grad_heads = weighted * inverse - heads * inverse * inverse * inverse * inner / heads.shape[-1]
    grad_keys = grad_heads.reshape(keys_student.shape).astype(jnp.bfloat16)
    grad_gain = jnp.sum(upstream * heads * inverse, axis=(0, 1))
    loss_total, gain_total = lax.psum((jnp.sum(differ * differ), grad_gain), "fsdp")
    tokens_all = hidden_in.shape[1] * lax.axis_size("fsdp")
    grad = lax.dot_general(
        normed_student, grad_keys, (((0,), (0,)), ((), ())), preferred_element_type=jnp.float32
    )
    grad_rows = lax.psum_scatter(grad, "fsdp", scatter_dimension=0, tiled=True)
    distill_loss = (loss_total / (tokens_all * w_key.shape[2])).reshape(1)
    return (grad_rows[None], gain_total[None], distill_loss)


def step(hidden_in, gain_in, w_key, key_gain, partner):
    body = plain if w_key.shape[1] % 128 else local
    return body(hidden_in, gain_in, w_key, key_gain, partner)


def solution(mesh):
    return jax.shard_map(
        step,
        mesh=mesh,
        in_specs=(P("mp", "fsdp", None), P("mp", None), P("mp", "fsdp", None), P("mp", None), P()),
        out_specs=(P("mp", "fsdp", None), P("mp", None), P("mp")),
        check_vma=False,
    )
```

```python
import functools

import jax
import jax.numpy as jnp
from jax import lax
from jax.experimental import pallas as pl
from jax.experimental.pallas import tpu as pltpu
from jax.sharding import PartitionSpec as P

EPS = 1e-06
NORM_TOKENS = 128
KEY_TOKENS = 256
LATE_TOKENS = 384
VMEM_LIMIT = 24 * 1024 * 1024
SHORT = pl.CostEstimate(flops=1, bytes_accessed=1, transcendentals=0)
ANY = pl.BlockSpec(memory_space=pl.ANY)
SMEM = pl.BlockSpec(memory_space=pltpu.SMEM)


def norm_kernel(order, rows, place_ref, hidden_ref, gain_ref, out_ref):
    values = hidden_ref[...].astype(jnp.float32)
    scale = lax.rsqrt(jnp.sum(values * values, axis=-1, keepdims=True) / values.shape[1] + EPS)
    line, member = lax.div(place_ref[0], 2), lax.rem(place_ref[0], 2)
    for at, (step, pair) in enumerate(order):
        owner = lax.rem(line + step, len(order) // 2) * 2 + lax.rem(member + pair, 2)
        source = pl.ds(pl.multiple_of(owner * rows, 128), rows)
        scaled = hidden_ref[:, source].astype(jnp.float32) * scale * gain_ref[:, source]
        out_ref[:, at * rows : (at + 1) * rows] = scaled.astype(jnp.bfloat16)


def normed_input(place, hidden, gain, order, rows):
    tokens, width = hidden.shape
    block = pl.BlockSpec((NORM_TOKENS, width), lambda i: (i, 0))
    return pl.pallas_call(
        functools.partial(norm_kernel, order, rows),
        grid=(tokens // NORM_TOKENS,),
        in_specs=[SMEM, block, pl.BlockSpec((1, width), lambda i: (0, 0))],
        out_specs=block,
        out_shape=pltpu.HBM(hidden.shape, jnp.bfloat16),
        compiler_params=pltpu.CompilerParams(vmem_limit_bytes=VMEM_LIMIT),
        cost_estimate=SHORT,
        name="norm_input",
    )(place, in_hbm(hidden), gain)


def copy_blocks(sources, target, sems):
    copies, at = [], 0
    for i, source in enumerate(sources):
        rows = source.shape[0]
        copies.append(pltpu.make_async_copy(source, target.at[pl.ds(at, rows)], sems.at[i]))
        at += rows
    for copy in copies:
        copy.start()
    return copies


def load_weights(choice_ref, choices, target, sems):
    def load(sources):
        for copy in copy_blocks(sources, target, sems):
            copy.wait()

    if len(choices) == 1:
        load(choices[0])
    else:
        for i, sources in enumerate(choices):
            pl.when(choice_ref[0] == i)(functools.partial(load, sources))


def in_hbm(array):
    return pltpu.with_memory_space_constraint(array, pltpu.HBM)


def split(refs, counts):
    lists = []
    for count in counts:
        lists.append(refs[:count])
        refs = refs[count:]
    return lists, refs


def pack_kernel(counts, choice_ref, *refs):
    choices, (out_ref, sems) = split(refs, counts)
    load_weights(choice_ref, choices, out_ref, sems)


def pack(choice, *choices):
    rows, wide = sum(block.shape[0] for block in choices[0]), choices[0][0].shape[1]
    counts = [len(blocks) for blocks in choices]
    return pl.pallas_call(
        functools.partial(pack_kernel, counts),
        in_specs=[SMEM] + [ANY] * sum(counts),
        out_specs=pl.BlockSpec(memory_space=pltpu.VMEM),
        out_shape=jax.ShapeDtypeStruct((rows, wide), choices[0][0].dtype),
        scratch_shapes=[pltpu.SemaphoreType.DMA((max(counts),))],
        compiler_params=pltpu.CompilerParams(vmem_limit_bytes=VMEM_LIMIT),
        cost_estimate=SHORT,
        name="pack_blocks",
    )(choice, *[block for blocks in choices for block in blocks])


def early_kernel(counts, adds, choice_ref, normed_ref, *refs):
    choices, refs = split(refs, counts)
    before, (keys_ref, weights, sems) = refs[:-3], refs[-3:]

    @pl.when(pl.program_id(0) == 0)
    def _():
        load_weights(choice_ref, choices, weights, sems)

    keys = jnp.dot(normed_ref[...], weights[...], preferred_element_type=jnp.float32)
    keys_ref[...] = keys + before[0][...] if adds else keys


def early_keys(choice, normed, choices, first, before=None):
    depth, wide, tokens = sum(block.shape[0] for block in choices[0]), choices[0][0].shape[1], normed.shape[0]
    counts = [len(blocks) for blocks in choices]
    keys = pl.BlockSpec((KEY_TOKENS, wide), lambda i: (i, 0))
    before = [] if before is None else [before]
    return pl.pallas_call(
        functools.partial(early_kernel, counts, bool(before)),
        grid=(tokens // KEY_TOKENS,),
        in_specs=[SMEM, pl.BlockSpec((KEY_TOKENS, depth), lambda i: (i, first // depth))]
        + [ANY] * sum(counts)
        + [keys] * len(before),
        out_specs=keys,
        out_shape=jax.ShapeDtypeStruct((tokens, wide), jnp.float32),
        scratch_shapes=[pltpu.VMEM((depth, wide), jnp.bfloat16), pltpu.SemaphoreType.DMA((max(counts),))],
        compiler_params=pltpu.CompilerParams(vmem_limit_bytes=VMEM_LIMIT),
        cost_estimate=SHORT,
        name="early_keys",
    )(choice, in_hbm(normed), *[block for blocks in choices for block in blocks], *before)


def late_kernel(counts, choice_ref, student_ref, teacher_ref, part_s_ref, part_t_ref, gain_s_ref, gain_t_ref, *refs):
    (same, *choices), refs = split(refs, counts)
    keep_of_ref, give_of_ref, grad_ref, stats_ref, keep_ref, give_ref, w_s, w_t, sems_s, sems_t = refs
    step = pl.program_id(0)
    head, features = gain_s_ref.shape[1], part_s_ref.shape[1]

    @pl.when(step == 0)
    def _():
        own = copy_blocks(same, w_s, sems_s)
        load_weights(choice_ref, choices, w_t, sems_t)
        for copy in own:
            copy.wait()

    keys_s = part_s_ref[...] + jnp.dot(student_ref[...], w_s[...], preferred_element_type=jnp.float32)
    keys_t = part_t_ref[...] + jnp.dot(teacher_ref[...], w_t[...], preferred_element_type=jnp.float32)
    gain_s, gain_t = gain_s_ref[...], gain_t_ref[...]
    gain_sum, loss_sum = 0.0, 0.0
    tokens = pl.ds(pl.multiple_of(step * keys_s.shape[0], 128), keys_s.shape[0])
    for at in range(0, features, head):
        heads, taught = keys_s[:, at : at + head], keys_t[:, at : at + head]
        inverse = lax.rsqrt(jnp.mean(heads * heads, axis=-1, keepdims=True) + EPS)
        inverse_t = lax.rsqrt(jnp.mean(taught * taught, axis=-1, keepdims=True) + EPS)
        differ = heads * inverse * gain_s - taught * inverse_t * gain_t
        upstream = differ * (1.0 / features)
        weighted = upstream * gain_s
        inner = jnp.sum(weighted * heads, axis=-1, keepdims=True)
        grad = weighted * inverse - heads * (inverse * inverse * inverse * inner / head)
        grad_ref[tokens, at : at + head] = grad.astype(jnp.bfloat16)
        gain_sum = gain_sum + jnp.sum(upstream * heads * inverse, axis=0, keepdims=True)
        loss_sum = loss_sum + jnp.sum(differ * differ, axis=0, keepdims=True)
    loss_sum = jnp.broadcast_to(jnp.sum(loss_sum, axis=1, keepdims=True), gain_sum.shape)
    stats = jnp.concatenate([gain_sum, loss_sum], axis=1)

    @pl.when(step == 0)
    def _():
        stats_ref[...] = stats

    @pl.when(step != 0)
    def _():
        stats_ref[...] += stats

    @pl.when(step == pl.num_programs(0) - 1)
    def _():
        for block_ref, out_ref in ((give_of_ref, give_ref), (keep_of_ref, keep_ref)):
            out_ref[...] = lax.dot_general(
                grad_ref[...], block_ref[...], (((0,), (0,)), ((), ())), preferred_element_type=jnp.float32
            ).astype(out_ref.dtype)


def late_keys(choice, student, teacher, part_s, part_t, gain_s, gain_t, same, choices, rows, far):
    counts, (tokens, wide), head = [len(same)] + [len(blocks) for blocks in choices], part_s.shape, gain_s.shape[1]
    depth = sum(block.shape[0] for block in same)
    last = student.shape[1] // depth - 1
    token_block = pl.BlockSpec((LATE_TOKENS, depth), lambda i: (i, last))
    keys = pl.BlockSpec((LATE_TOKENS, wide), lambda i: (i, 0))
    gain = pl.BlockSpec((1, head), lambda i: (0, 0))
    far_blocks = [pl.BlockSpec((tokens, rows), lambda i, at=at: (0, at)) for at in far]
    outs = [
        jax.ShapeDtypeStruct((tokens, wide), jnp.bfloat16),
        jax.ShapeDtypeStruct((1, 2 * head), jnp.float32),
        jax.ShapeDtypeStruct((wide, rows), jnp.float32),
        jax.ShapeDtypeStruct((wide, rows), jnp.bfloat16),
    ]
    student, teacher = in_hbm(student), in_hbm(teacher)
    return pl.pallas_call(
        functools.partial(late_kernel, counts),
        grid=(tokens // LATE_TOKENS,),
        in_specs=[SMEM, token_block, token_block, keys, keys, gain, gain] + [ANY] * sum(counts) + far_blocks,
        out_specs=[pl.BlockSpec(out.shape, lambda i: (0, 0)) for out in outs],
        out_shape=outs,
        scratch_shapes=[pltpu.VMEM((depth, wide), jnp.bfloat16)] * 2
        + [pltpu.SemaphoreType.DMA((count,)) for count in (counts[0], max(counts[1:]))],
        compiler_params=pltpu.CompilerParams(vmem_limit_bytes=VMEM_LIMIT),
        cost_estimate=SHORT,
        name="late_keys",
    )(
        choice,
        student,
        teacher,
        part_s,
        part_t,
        gain_s,
        gain_t,
        *same,
        *[block for blocks in choices for block in blocks],
        student,
        student,
    )


def grad_kernel(grad_ref, student_ref, out_ref):
    out_ref[0] = lax.dot_general(
        grad_ref[...], student_ref[...], (((0,), (0,)), ((), ())), preferred_element_type=jnp.float32
    ).astype(out_ref.dtype)


def grad_blocks(grad_keys, student, rows, blocks, dtype):
    (tokens, wide), count, first = grad_keys.shape, len(blocks), blocks[0]
    stride = blocks[1] - first if count > 1 else 1
    return pl.pallas_call(
        grad_kernel,
        grid=(count,),
        in_specs=[
            pl.BlockSpec((tokens, wide), lambda i: (0, 0)),
            pl.BlockSpec((tokens, rows), lambda i: (0, first + stride * i)),
        ],
        out_specs=pl.BlockSpec((1, wide, rows), lambda i: (i, 0, 0)),
        out_shape=jax.ShapeDtypeStruct((count, wide, rows), dtype),
        compiler_params=pltpu.CompilerParams(vmem_limit_bytes=VMEM_LIMIT),
        cost_estimate=SHORT,
        name="grad_blocks",
    )(grad_keys, in_hbm(student))


def swap(value, axis, bit):
    return lax.ppermute(value, axis, [(i, i ^ bit) for i in range(lax.axis_size(axis))])


def fetch(value, step):
    size = lax.axis_size("fsdp")
    return lax.ppermute(value, "fsdp", [(i, (i - 2 * step) % size) for i in range(size)])


def after(value, *others):
    return lax.optimization_barrier((value,) + others)[0]


def phase(*values):
    return lax.optimization_barrier(values)


def local(hidden_in, gain_in, w_key, key_gain, partner):
    own_index = lax.axis_index("mp")
    teacher = partner[own_index]
    place = lax.axis_index("fsdp")
    lines = lax.axis_size("fsdp") // 2
    tok_rows, width = hidden_in.shape[1:]
    rows, features = w_key.shape[1:]
    head = key_gain.shape[1]

    far = lines // 2
    near = [step for step in range(1, lines) if step != far]
    order = [(0, 0), (0, 1)] + [(step, 0) for step in near]
    order += [(step, 1) for step in near[:-1]] + [(far, 0), (near[-1], 1), (far, 1)]
    place = place.astype(jnp.int32).reshape(1)
    own = w_key[0]

    same, other = {(0, 0): own}, {}
    for step in near:
        same[step, 0] = fetch(own, step)
    same[0, 1] = swap(own, "fsdp", 1)
    flags = [teacher == own_index ^ 2, teacher == own_index ^ 1, partner[own_index ^ 1] == own_index]
    choice, across, offer = [jnp.where(flag, 0, 1).astype(jnp.int32).reshape(1) for flag in flags]
    other[0, 0] = swap(after(own, choice), "mp", 2)
    other[0, 1] = swap(same[0, 1], "mp", 2)
    same[far, 0] = fetch(after(own, same[near[0], 0]), far)
    place, choice, across, offer = phase(place, choice, across, offer)
    student = normed_input(place, hidden_in[0], gain_in.astype(jnp.float32), order, rows)
    gains_own = jnp.concatenate([gain_in, key_gain], axis=1)
    gains_beside = swap(gains_own, "mp", 2)
    student, gains_beside, other[0, 0], other[0, 1], *moved = phase(
        student, gains_beside, other[0, 0], other[0, 1], *[same[step, 0] for step in near]
    )
    gains_same = jnp.concatenate([gains_own, gains_beside], axis=0)
    gains_cross = swap(gains_same, "mp", 1)
    gains_teacher = jnp.where(
        choice == 0, gains_same[1:], jnp.where(across == 0, gains_cross[:1], gains_cross[1:])
    ).astype(jnp.float32)
    normed = normed_input(place, after(hidden_in[0], student), gains_teacher[:, :width], order, rows)

    for step, block in zip(near, moved):
        same[step, 0] = block
        other[step, 0] = swap(block, "mp", 2)
        same[step, 1] = swap(block, "fsdp", 1)
    same[far, 1] = fetch(after(same[0, 1], other[near[0], 0], same[near[0], 1]), far)

    arrived = phase(
        same[far, 0],
        normed,
        *[same[step, 1] for step in near],
        *[other[step, 0] for step in near],
    )
    same[far, 0], normed = arrived[:2]
    for i, step in enumerate(near):
        same[step, 1], other[step, 0] = arrived[2 + i], arrived[2 + len(near) + i]
    other[far, 0] = swap(same[far, 0], "mp", 2)
    for i, step in enumerate(near):
        other[step, 1] = swap(other[step, 0], "fsdp", 1) if i % 2 == 0 else swap(same[step, 1], "mp", 2)

    def cross(keys, *wait):
        return swap(pack(after(offer, *wait), [same[key] for key in keys], [other[key] for key in keys]), "mp", 1)

    first, second, third = order[: 2 + len(near)], order[2 + len(near) : -2], order[-2:]
    part_s = early_keys(choice, student, [[same[key] for key in first + second]], 0)
    other[far, 1] = swap(after(other[far, 0], part_s), "fsdp", 1)
    part_t = early_keys(choice, normed, [[other[key] for key in first], [cross(first)]], 0)
    crossed = cross(third, part_t)
    part_t = early_keys(choice, normed, [[other[key] for key in second], [cross(second)]], len(first) * rows, part_t)
    grad_keys, stats, keep_far, give_far = late_keys(
        choice,
        student,
        normed,
        part_s,
        part_t,
        key_gain.astype(jnp.float32),
        gains_teacher[:, width:],
        [same[key] for key in third],
        [[other[key] for key in third], [crossed]],
        rows,
        [order.index((far, pair)) for pair in range(2)],
    )

    wide = features // 2

    def grads(keys, dtype, *wait):
        return grad_blocks(after(grad_keys, *wait), student, rows, [order.index(key) for key in keys], dtype)

    sums, bit, first_step = stats[0], 2, None
    while bit < lax.axis_size("fsdp"):
        sums = sums + swap(sums, "fsdp", bit)
        first_step = sums if first_step is None else first_step
        bit *= 2
    given = [swap(give_far[:wide], "fsdp", 1), swap(after(give_far[wide:], first_step), "fsdp", 1)]
    pieces = grads([(step, 1) for step in near], jnp.bfloat16, given[0])
    keep = grads([(step, 0) for step in near], jnp.float32, pieces)
    ends = grads([(0, 0), (0, 1)], jnp.float32, keep)
    kept = [keep_far[i * wide : (i + 1) * wide] for i in range(2)] + [keep[i] for i in range(len(near))]
    arrived = []
    for at, step in enumerate([far, far] + near):
        if at >= 2:
            ready = given[0] if at == 2 else arrived[at - 3]
            given.append(swap(after(pieces[at - 2], ready), "fsdp", 1))
        mine, block = phase(kept[at], given[at])
        summed = (mine + block.astype(jnp.float32)).astype(jnp.bfloat16)
        arrived.append(fetch(after(summed, [summed, sums, *arrived][at]), -step))
    last = swap(after(ends[1].astype(jnp.bfloat16), given[2], arrived[1]), "fsdp", 1)
    sums = sums + swap(after(sums, given[-1]), "fsdp", 1)
    total = ends[0] + last.astype(jnp.float32) + jnp.concatenate(arrived[:2], axis=0).astype(jnp.float32)
    for block in arrived[2:]:
        total = total + block.astype(jnp.float32)

    tokens_all = tok_rows * lax.axis_size("fsdp")
    distill_loss = (sums[head] / (tokens_all * features)).reshape(1)
    return (total.T[None], sums[None, :head], distill_loss)


def norm_input(hidden, gain):
    values = hidden.astype(jnp.float32)
    scale = lax.rsqrt(jnp.mean(values * values, axis=-1, keepdims=True) + EPS)
    return (values * scale * gain.astype(jnp.float32)).astype(jnp.bfloat16)


def norm_keys(keys, gain):
    heads = keys.reshape(keys.shape[0], -1, gain.shape[0])
    inverse = lax.rsqrt(jnp.mean(heads * heads, axis=-1, keepdims=True) + EPS)
    return (heads, inverse, heads * inverse * gain.astype(jnp.float32))


def plain(hidden_in, gain_in, w_key, key_gain, partner):
    partner_index = partner[lax.axis_index("mp")]
    every = [lax.all_gather(array, "mp", axis=0, tiled=True) for array in (w_key, gain_in, key_gain)]
    teach_w, teach_gain, teach_key_gain = [
        lax.dynamic_index_in_dim(array, partner_index, 0, keepdims=False) for array in every
    ]
    normed_student = norm_input(hidden_in[0], gain_in[0])
    normed_teacher = norm_input(hidden_in[0], teach_gain)
    keys_student, keys_teacher = [
        jnp.dot(normed, lax.all_gather(weight, "fsdp", axis=0, tiled=True), preferred_element_type=jnp.float32)
        for normed, weight in ((normed_student, w_key[0]), (normed_teacher, teach_w))
    ]
    heads, inverse, out_student = norm_keys(keys_student, key_gain[0])
    differ = out_student - norm_keys(keys_teacher, teach_key_gain)[2]
    upstream = differ / w_key.shape[2]
    weighted = upstream * key_gain[0].astype(jnp.float32)
    inner = jnp.sum(weighted * heads, axis=-1, keepdims=True)
    grad_heads = weighted * inverse - heads * inverse * inverse * inverse * inner / heads.shape[-1]
    grad_keys = grad_heads.reshape(keys_student.shape).astype(jnp.bfloat16)
    grad_gain = jnp.sum(upstream * heads * inverse, axis=(0, 1))
    loss_total, gain_total = lax.psum((jnp.sum(differ * differ), grad_gain), "fsdp")
    tokens_all = hidden_in.shape[1] * lax.axis_size("fsdp")
    grad = lax.dot_general(
        normed_student, grad_keys, (((0,), (0,)), ((), ())), preferred_element_type=jnp.float32
    )
    grad_rows = lax.psum_scatter(grad, "fsdp", scatter_dimension=0, tiled=True)
    distill_loss = (loss_total / (tokens_all * w_key.shape[2])).reshape(1)
    return (grad_rows[None], gain_total[None], distill_loss)


def step(hidden_in, gain_in, w_key, key_gain, partner):
    body = plain if w_key.shape[1] % 128 else local
    return body(hidden_in, gain_in, w_key, key_gain, partner)


def solution(mesh):
    return jax.shard_map(
        step,
        mesh=mesh,
        in_specs=(P("mp", "fsdp", None), P("mp", None), P("mp", "fsdp", None), P("mp", None), P()),
        out_specs=(P("mp", "fsdp", None), P("mp", None), P("mp")),
        check_vma=False,
    )
```

```python
import functools

import jax
import jax.numpy as jnp
from jax import lax
from jax.experimental import pallas as pl
from jax.experimental.pallas import tpu as pltpu
from jax.sharding import PartitionSpec as P

EPS = 1e-06
NORM_TOKENS = 128
KEY_TOKENS = 256
VMEM_LIMIT = 24 * 1024 * 1024
SHORT = pl.CostEstimate(flops=1, bytes_accessed=1, transcendentals=0)
ANY = pl.BlockSpec(memory_space=pl.ANY)
SMEM = pl.BlockSpec(memory_space=pltpu.SMEM)


def norm_kernel(order, rows, place_ref, hidden_ref, gain_ref, out_ref):
    values = hidden_ref[...].astype(jnp.float32)
    scale = lax.rsqrt(jnp.sum(values * values, axis=-1, keepdims=True) / values.shape[1] + EPS)
    line, member = lax.div(place_ref[0], 2), lax.rem(place_ref[0], 2)
    for at, (step, pair) in enumerate(order):
        owner = lax.rem(line + step, len(order) // 2) * 2 + lax.rem(member + pair, 2)
        source = pl.ds(pl.multiple_of(owner * rows, 128), rows)
        scaled = hidden_ref[:, source].astype(jnp.float32) * scale * gain_ref[:, source]
        out_ref[:, at * rows : (at + 1) * rows] = scaled.astype(jnp.bfloat16)


def normed_input(place, hidden, gain, order, rows):
    tokens, width = hidden.shape
    block = pl.BlockSpec((NORM_TOKENS, width), lambda i: (i, 0))
    return pl.pallas_call(
        functools.partial(norm_kernel, order, rows),
        grid=(tokens // NORM_TOKENS,),
        in_specs=[SMEM, block, pl.BlockSpec((1, width), lambda i: (0, 0))],
        out_specs=block,
        out_shape=pltpu.HBM(hidden.shape, jnp.bfloat16),
        compiler_params=pltpu.CompilerParams(vmem_limit_bytes=VMEM_LIMIT),
        cost_estimate=SHORT,
        name="norm_input",
    )(place, in_hbm(hidden), gain)


def copy_blocks(sources, target, sems):
    copies, at = [], 0
    for i, source in enumerate(sources):
        rows = source.shape[0]
        copies.append(pltpu.make_async_copy(source, target.at[pl.ds(at, rows)], sems.at[i]))
        at += rows
    for copy in copies:
        copy.start()
    return copies


def load_weights(choice_ref, choices, target, sems):
    def load(sources):
        for copy in copy_blocks(sources, target, sems):
            copy.wait()

    if len(choices) == 1:
        load(choices[0])
    else:
        for i, sources in enumerate(choices):
            pl.when(choice_ref[0] == i)(functools.partial(load, sources))


def in_hbm(array):
    return pltpu.with_memory_space_constraint(array, pltpu.HBM)


def split(refs, counts):
    lists = []
    for count in counts:
        lists.append(refs[:count])
        refs = refs[count:]
    return lists, refs


def pack_kernel(counts, choice_ref, *refs):
    choices, (out_ref, sems) = split(refs, counts)
    load_weights(choice_ref, choices, out_ref, sems)


def pack(choice, *choices):
    rows, wide = sum(block.shape[0] for block in choices[0]), choices[0][0].shape[1]
    counts = [len(blocks) for blocks in choices]
    return pl.pallas_call(
        functools.partial(pack_kernel, counts),
        in_specs=[SMEM] + [ANY] * sum(counts),
        out_specs=pl.BlockSpec(memory_space=pltpu.VMEM),
        out_shape=jax.ShapeDtypeStruct((rows, wide), choices[0][0].dtype),
        scratch_shapes=[pltpu.SemaphoreType.DMA((max(counts),))],
        compiler_params=pltpu.CompilerParams(vmem_limit_bytes=VMEM_LIMIT),
        cost_estimate=SHORT,
        name="pack_blocks",
    )(choice, *[block for blocks in choices for block in blocks])


def early_kernel(counts, adds, choice_ref, normed_ref, *refs):
    choices, refs = split(refs, counts)
    before, (keys_ref, weights, sems) = refs[:-3], refs[-3:]

    @pl.when(pl.program_id(0) == 0)
    def _():
        load_weights(choice_ref, choices, weights, sems)

    keys = jnp.dot(normed_ref[...], weights[...], preferred_element_type=jnp.float32)
    keys_ref[...] = keys + before[0][...] if adds else keys


def early_keys(choice, normed, choices, first, before=None):
    depth, wide, tokens = sum(block.shape[0] for block in choices[0]), choices[0][0].shape[1], normed.shape[0]
    counts = [len(blocks) for blocks in choices]
    keys = pl.BlockSpec((KEY_TOKENS, wide), lambda i: (i, 0))
    before = [] if before is None else [before]
    return pl.pallas_call(
        functools.partial(early_kernel, counts, bool(before)),
        grid=(tokens // KEY_TOKENS,),
        in_specs=[SMEM, pl.BlockSpec((KEY_TOKENS, depth), lambda i: (i, first // depth))]
        + [ANY] * sum(counts)
        + [keys] * len(before),
        out_specs=keys,
        out_shape=jax.ShapeDtypeStruct((tokens, wide), jnp.float32),
        scratch_shapes=[pltpu.VMEM((depth, wide), jnp.bfloat16), pltpu.SemaphoreType.DMA((max(counts),))],
        compiler_params=pltpu.CompilerParams(vmem_limit_bytes=VMEM_LIMIT),
        cost_estimate=SHORT,
        name="early_keys",
    )(choice, in_hbm(normed), *[block for blocks in choices for block in blocks], *before)


def late_kernel(counts, choice_ref, student_ref, teacher_ref, part_s_ref, part_t_ref, gain_s_ref, gain_t_ref, *refs):
    (same, *choices), refs = split(refs, counts)
    keep_of_ref, give_of_ref, grad_ref, stats_ref, keep_ref, give_ref, w_s, w_t, sems_s, sems_t = refs
    step = pl.program_id(0)
    head, features = gain_s_ref.shape[1], part_s_ref.shape[1]

    @pl.when(step == 0)
    def _():
        own = copy_blocks(same, w_s, sems_s)
        load_weights(choice_ref, choices, w_t, sems_t)
        for copy in own:
            copy.wait()

    keys_s = part_s_ref[...] + jnp.dot(student_ref[...], w_s[...], preferred_element_type=jnp.float32)
    keys_t = part_t_ref[...] + jnp.dot(teacher_ref[...], w_t[...], preferred_element_type=jnp.float32)
    gain_s, gain_t = gain_s_ref[...], gain_t_ref[...]
    gain_sum, loss_sum = 0.0, 0.0
    tokens = pl.ds(pl.multiple_of(step * keys_s.shape[0], 256), keys_s.shape[0])
    for at in range(0, features, head):
        heads, taught = keys_s[:, at : at + head], keys_t[:, at : at + head]
        inverse = lax.rsqrt(jnp.mean(heads * heads, axis=-1, keepdims=True) + EPS)
        inverse_t = lax.rsqrt(jnp.mean(taught * taught, axis=-1, keepdims=True) + EPS)
        differ = heads * inverse * gain_s - taught * inverse_t * gain_t
        upstream = differ * (1.0 / features)
        weighted = upstream * gain_s
        inner = jnp.sum(weighted * heads, axis=-1, keepdims=True)
        grad = weighted * inverse - heads * (inverse * inverse * inverse * inner / head)
        grad_ref[tokens, at : at + head] = grad.astype(jnp.bfloat16)
        gain_sum = gain_sum + jnp.sum(upstream * heads * inverse, axis=0, keepdims=True)
        loss_sum = loss_sum + jnp.sum(differ * differ, axis=0, keepdims=True)
    loss_sum = jnp.broadcast_to(jnp.sum(loss_sum, axis=1, keepdims=True), gain_sum.shape)
    stats = jnp.concatenate([gain_sum, loss_sum], axis=1)

    @pl.when(step == 0)
    def _():
        stats_ref[...] = stats

    @pl.when(step != 0)
    def _():
        stats_ref[...] += stats

    @pl.when(step == pl.num_programs(0) - 1)
    def _():
        for block_ref, out_ref in ((give_of_ref, give_ref), (keep_of_ref, keep_ref)):
            out_ref[...] = lax.dot_general(
                grad_ref[...], block_ref[...], (((0,), (0,)), ((), ())), preferred_element_type=jnp.float32
            ).astype(out_ref.dtype)


def late_keys(choice, student, teacher, part_s, part_t, gain_s, gain_t, same, choices, rows, far):
    counts, (tokens, wide), head = [len(same)] + [len(blocks) for blocks in choices], part_s.shape, gain_s.shape[1]
    depth = sum(block.shape[0] for block in same)
    last = student.shape[1] // depth - 1
    token_block = pl.BlockSpec((KEY_TOKENS, depth), lambda i: (i, last))
    keys = pl.BlockSpec((KEY_TOKENS, wide), lambda i: (i, 0))
    gain = pl.BlockSpec((1, head), lambda i: (0, 0))
    far_blocks = [pl.BlockSpec((tokens, rows), lambda i, at=at: (0, at)) for at in far]
    outs = [
        jax.ShapeDtypeStruct((tokens, wide), jnp.bfloat16),
        jax.ShapeDtypeStruct((1, 2 * head), jnp.float32),
        jax.ShapeDtypeStruct((wide, rows), jnp.float32),
        jax.ShapeDtypeStruct((wide, rows), jnp.bfloat16),
    ]
    student, teacher = in_hbm(student), in_hbm(teacher)
    return pl.pallas_call(
        functools.partial(late_kernel, counts),
        grid=(tokens // KEY_TOKENS,),
        in_specs=[SMEM, token_block, token_block, keys, keys, gain, gain] + [ANY] * sum(counts) + far_blocks,
        out_specs=[pl.BlockSpec(out.shape, lambda i: (0, 0)) for out in outs],
        out_shape=outs,
        scratch_shapes=[pltpu.VMEM((depth, wide), jnp.bfloat16)] * 2
        + [pltpu.SemaphoreType.DMA((count,)) for count in (counts[0], max(counts[1:]))],
        compiler_params=pltpu.CompilerParams(vmem_limit_bytes=VMEM_LIMIT),
        cost_estimate=SHORT,
        name="late_keys",
    )(
        choice,
        student,
        teacher,
        part_s,
        part_t,
        gain_s,
        gain_t,
        *same,
        *[block for blocks in choices for block in blocks],
        student,
        student,
    )


def grad_kernel(grad_ref, student_ref, out_ref):
    out_ref[0] = lax.dot_general(
        grad_ref[...], student_ref[...], (((0,), (0,)), ((), ())), preferred_element_type=jnp.float32
    ).astype(out_ref.dtype)


def grad_blocks(grad_keys, student, rows, blocks, dtype):
    (tokens, wide), count, first = grad_keys.shape, len(blocks), blocks[0]
    stride = blocks[1] - first if count > 1 else 1
    return pl.pallas_call(
        grad_kernel,
        grid=(count,),
        in_specs=[
            pl.BlockSpec((tokens, wide), lambda i: (0, 0)),
            pl.BlockSpec((tokens, rows), lambda i: (0, first + stride * i)),
        ],
        out_specs=pl.BlockSpec((1, wide, rows), lambda i: (i, 0, 0)),
        out_shape=jax.ShapeDtypeStruct((count, wide, rows), dtype),
        compiler_params=pltpu.CompilerParams(vmem_limit_bytes=VMEM_LIMIT),
        cost_estimate=SHORT,
        name="grad_blocks",
    )(grad_keys, in_hbm(student))


def swap(value, axis, bit):
    return lax.ppermute(value, axis, [(i, i ^ bit) for i in range(lax.axis_size(axis))])


def fetch(value, step):
    size = lax.axis_size("fsdp")
    return lax.ppermute(value, "fsdp", [(i, (i - 2 * step) % size) for i in range(size)])


def after(value, *others):
    return lax.optimization_barrier((value,) + others)[0]


def phase(*values):
    return lax.optimization_barrier(values)


def local(hidden_in, gain_in, w_key, key_gain, partner):
    own_index = lax.axis_index("mp")
    teacher = partner[own_index]
    place = lax.axis_index("fsdp")
    lines = lax.axis_size("fsdp") // 2
    tok_rows, width = hidden_in.shape[1:]
    rows, features = w_key.shape[1:]
    head = key_gain.shape[1]

    far = lines // 2
    near = [step for step in range(1, lines) if step != far]
    order = [(0, 0), (0, 1)] + [(step, 0) for step in near]
    order += [(step, 1) for step in near[:-1]] + [(far, 0), (near[-1], 1), (far, 1)]
    place = place.astype(jnp.int32).reshape(1)
    own = w_key[0]

    same, other = {(0, 0): own}, {}
    for step in near:
        same[step, 0] = fetch(own, step)
    same[0, 1] = swap(own, "fsdp", 1)
    other[0, 0] = swap(own, "mp", 2)
    other[0, 1] = swap(same[0, 1], "mp", 2)
    same[far, 0] = fetch(after(own, same[near[0], 0]), far)
    flags = [teacher == own_index ^ 2, teacher == own_index ^ 1, partner[own_index ^ 1] == own_index]
    choice, across, offer = [jnp.where(flag, 0, 1).astype(jnp.int32).reshape(1) for flag in flags]
    place, choice, across, offer = phase(place, choice, across, offer)
    student = normed_input(place, hidden_in[0], gain_in.astype(jnp.float32), order, rows)
    gains_own = jnp.concatenate([gain_in, key_gain], axis=1)
    gains_beside = swap(gains_own, "mp", 2)
    student, other[0, 0], other[0, 1], *moved = phase(
        student, other[0, 0], other[0, 1], *[same[step, 0] for step in near]
    )
    gains_same = jnp.concatenate([gains_own, gains_beside], axis=0)
    gains_cross = swap(gains_same, "mp", 1)
    gains_teacher = jnp.where(
        choice == 0, gains_same[1:], jnp.where(across == 0, gains_cross[:1], gains_cross[1:])
    ).astype(jnp.float32)
    normed = normed_input(place, after(hidden_in[0], student), gains_teacher[:, :width], order, rows)

    for step, block in zip(near, moved):
        same[step, 0] = block
        other[step, 0] = swap(block, "mp", 2)
        same[step, 1] = swap(block, "fsdp", 1)
    same[far, 1] = fetch(after(same[0, 1], other[near[0], 0], same[near[0], 1]), far)

    arrived = phase(
        same[far, 0],
        normed,
        *[same[step, 1] for step in near],
        *[other[step, 0] for step in near],
    )
    same[far, 0], normed = arrived[:2]
    for i, step in enumerate(near):
        same[step, 1], other[step, 0] = arrived[2 + i], arrived[2 + len(near) + i]
    other[far, 0] = swap(same[far, 0], "mp", 2)
    for i, step in enumerate(near):
        other[step, 1] = swap(other[step, 0], "fsdp", 1) if i % 2 == 0 else swap(same[step, 1], "mp", 2)

    def cross(keys, *wait):
        return swap(pack(after(offer, *wait), [same[key] for key in keys], [other[key] for key in keys]), "mp", 1)

    first, second, third = order[: 2 + len(near)], order[2 + len(near) : -2], order[-2:]
    part_s = early_keys(choice, student, [[same[key] for key in first + second]], 0)
    other[far, 1] = swap(after(other[far, 0], part_s), "fsdp", 1)
    part_t = early_keys(choice, normed, [[other[key] for key in first], [cross(first)]], 0)
    crossed = cross(third, part_t)
    part_t = early_keys(choice, normed, [[other[key] for key in second], [cross(second)]], len(first) * rows, part_t)
    grad_keys, stats, keep_far, give_far = late_keys(
        choice,
        student,
        normed,
        part_s,
        part_t,
        key_gain.astype(jnp.float32),
        gains_teacher[:, width:],
        [same[key] for key in third],
        [[other[key] for key in third], [crossed]],
        rows,
        [order.index((far, pair)) for pair in range(2)],
    )

    wide = features // 2

    def grads(keys, dtype, *wait):
        return grad_blocks(after(grad_keys, *wait), student, rows, [order.index(key) for key in keys], dtype)

    sums, bit, first_step = stats[0], 2, None
    while bit < lax.axis_size("fsdp"):
        sums = sums + swap(sums, "fsdp", bit)
        first_step = sums if first_step is None else first_step
        bit *= 2
    given = [swap(give_far[:wide], "fsdp", 1), swap(after(give_far[wide:], first_step), "fsdp", 1)]
    pieces = grads([(step, 1) for step in near], jnp.bfloat16, given[0])
    keep = grads([(step, 0) for step in near], jnp.float32, pieces)
    ends = grads([(0, 0), (0, 1)], jnp.float32, keep)
    kept = [keep_far[i * wide : (i + 1) * wide] for i in range(2)] + [keep[i] for i in range(len(near))]
    arrived = []
    for at, step in enumerate([far, far] + near):
        if at >= 2:
            ready = given[0] if at == 2 else arrived[at - 3]
            given.append(swap(after(pieces[at - 2], ready), "fsdp", 1))
        mine, block = phase(kept[at], given[at])
        summed = (mine + block.astype(jnp.float32)).astype(jnp.bfloat16)
        arrived.append(fetch(after(summed, [summed, sums, *arrived][at]), -step))
    last = swap(after(ends[1].astype(jnp.bfloat16), given[2], arrived[1]), "fsdp", 1)
    sums = sums + swap(after(sums, given[-1]), "fsdp", 1)
    total = ends[0] + last.astype(jnp.float32) + jnp.concatenate(arrived[:2], axis=0).astype(jnp.float32)
    for block in arrived[2:]:
        total = total + block.astype(jnp.float32)

    tokens_all = tok_rows * lax.axis_size("fsdp")
    distill_loss = (sums[head] / (tokens_all * features)).reshape(1)
    return (total.T[None], sums[None, :head], distill_loss)


def norm_input(hidden, gain):
    values = hidden.astype(jnp.float32)
    scale = lax.rsqrt(jnp.mean(values * values, axis=-1, keepdims=True) + EPS)
    return (values * scale * gain.astype(jnp.float32)).astype(jnp.bfloat16)


def norm_keys(keys, gain):
    heads = keys.reshape(keys.shape[0], -1, gain.shape[0])
    inverse = lax.rsqrt(jnp.mean(heads * heads, axis=-1, keepdims=True) + EPS)
    return (heads, inverse, heads * inverse * gain.astype(jnp.float32))


def plain(hidden_in, gain_in, w_key, key_gain, partner):
    partner_index = partner[lax.axis_index("mp")]
    every = [lax.all_gather(array, "mp", axis=0, tiled=True) for array in (w_key, gain_in, key_gain)]
    teach_w, teach_gain, teach_key_gain = [
        lax.dynamic_index_in_dim(array, partner_index, 0, keepdims=False) for array in every
    ]
    normed_student = norm_input(hidden_in[0], gain_in[0])
    normed_teacher = norm_input(hidden_in[0], teach_gain)
    keys_student, keys_teacher = [
        jnp.dot(normed, lax.all_gather(weight, "fsdp", axis=0, tiled=True), preferred_element_type=jnp.float32)
        for normed, weight in ((normed_student, w_key[0]), (normed_teacher, teach_w))
    ]
    heads, inverse, out_student = norm_keys(keys_student, key_gain[0])
    differ = out_student - norm_keys(keys_teacher, teach_key_gain)[2]
    upstream = differ / w_key.shape[2]
    weighted = upstream * key_gain[0].astype(jnp.float32)
    inner = jnp.sum(weighted * heads, axis=-1, keepdims=True)
    grad_heads = weighted * inverse - heads * inverse * inverse * inverse * inner / heads.shape[-1]
    grad_keys = grad_heads.reshape(keys_student.shape).astype(jnp.bfloat16)
    grad_gain = jnp.sum(upstream * heads * inverse, axis=(0, 1))
    loss_total, gain_total = lax.psum((jnp.sum(differ * differ), grad_gain), "fsdp")
    tokens_all = hidden_in.shape[1] * lax.axis_size("fsdp")
    grad = lax.dot_general(
        normed_student, grad_keys, (((0,), (0,)), ((), ())), preferred_element_type=jnp.float32
    )
    grad_rows = lax.psum_scatter(grad, "fsdp", scatter_dimension=0, tiled=True)
    distill_loss = (loss_total / (tokens_all * w_key.shape[2])).reshape(1)
    return (grad_rows[None], gain_total[None], distill_loss)


def step(hidden_in, gain_in, w_key, key_gain, partner):
    body = plain if w_key.shape[1] % 128 else local
    return body(hidden_in, gain_in, w_key, key_gain, partner)


def solution(mesh):
    return jax.shard_map(
        step,
        mesh=mesh,
        in_specs=(P("mp", "fsdp", None), P("mp", None), P("mp", "fsdp", None), P("mp", None), P()),
        out_specs=(P("mp", "fsdp", None), P("mp", None), P("mp")),
        check_vma=False,
    )
```
